256 devices in a mesh: scen: 16 (over y_lo, z), area: 16 (over y_hi, x, core).
Axes of the slice: x: 4, y: 4 (y_hi: 2, y_lo: 2; y = y_hi * 2 + y_lo), z: 8, core: 2. Of those that a mesh axis runs over, the one named last changes fastest.
Arguments:
- wind: bfloat16 [16, 24, 24576], P('scen', None, 'area'), may hold values from -4 to 4
- load: bfloat16 [24, 24576], P(None, 'area'), may hold values from 0 to 1.5
- ptdf_tiles: bfloat16 [128, 32, 128, 128], P('area'), may hold values from -0.09375 to 0.09375
- tile_cols: int32 [128, 32], P('area'), may hold values from 0 to 191, as said below
- line_cap: float32 [16384], P('area'), may hold values from 0.3 to 3
- gen_bus: int32 [4096], P('area'), may hold values from 0 to 24575, as said below
- gen_data: float32 [4, 4096], P(None, 'area'), may hold values from 0.05 to 18, as said below
- prob_weight: int32 [16], P('scen'), may hold values from 1 to 16
Outputs:
- commit_mean: float32 [24, 4096], P(None, 'area')
- dispatch_mean: float32 [24, 4096], P(None, 'area')
- dispatch: float32 [16, 24, 4096], P('scen', None, 'area')
- line_flow: float32 [16, 24, 16384], P('scen', None, 'area')
The draws below stay inside these ranges and needn't reach their ends.
Inputs may be any that keep to these rules, and one draw needn't show every extreme that they name: `tile_cols`: the 32 bus tiles of one row of line tiles are distinct. `gen_bus`: generator g stands at a bus of area g // 256, that is among buses (g // 256) * 1536 to (g // 256 + 1) * 1536 - 1. `gen_data`: linear cost 0.5 to 2, quadratic cost 0.05 to 0.5, commitment cost 0.2 to 1, capacity 2 to 18.
All inputs are finite; a program needn't handle non-finite values.
Results may differ from the reference program's by a relative error of at most 0.003.
Values may be sent and summed in bfloat16 or wider, within the bound.
No kernel may reach another device: no remote copies, remote signals or barrier semaphores. Data moves between devices by JAX's collectives and lax.ppermute only.
A program may use at most 64 MiB of HBM per device.

```python
import math
import jax
import jax.numpy as jnp
from jax import lax

BUSES = 24576
LINES = 16384
GENS = 4096
HOURS = 24
TILE = 128
NZ = 32
ITERS = 2
STEPS = 2
SCENS = 16
B_DEV = 1536
G_DEV = 256
N_AREA = 16


def draw_tile_cols(key, part):
    bus_tiles = BUSES // TILE
    row_keys = jax.random.split(jax.random.fold_in(key, 11), LINES // TILE)
    orders = jax.vmap(lambda subkey: jax.random.permutation(subkey, bus_tiles))(row_keys)
    return orders[:, :NZ].astype(jnp.int32)


def draw_gen_bus(key, part):
    owner = jnp.arange(GENS, dtype=jnp.int32) // G_DEV
    offset = jax.random.randint(jax.random.fold_in(key, 23), (GENS,), 0, B_DEV).astype(jnp.int32)
    offset = offset.at[0].set(0).at[GENS - 1].set(B_DEV - 1)
    return (owner * B_DEV + offset).astype(jnp.int32)


def draw_gen_data(key, part):
    keys = jax.random.split(jax.random.fold_in(key, 37), 4)
    linear = jax.random.uniform(keys[0], (GENS,), jnp.float32, 0.5, 2.0)
    quadratic = jnp.exp(jax.random.uniform(keys[1], (GENS,), jnp.float32, jnp.log(0.05), jnp.log(0.5)))
    fixed_cost = jax.random.uniform(keys[2], (GENS,), jnp.float32, 0.2, 1.0)
    capacity = jnp.exp(jax.random.uniform(keys[3], (GENS,), jnp.float32, jnp.log(2.0), jnp.log(18.0)))
    return jnp.stack([linear, quadratic, fixed_cost, capacity]).astype(jnp.float32)


def touch_ends(values, stream_key, smallest, high):
    place = [jax.random.randint(jax.random.fold_in(stream_key, axis), (), 0, length) for axis, length in enumerate(values.shape)]
    longest = values.shape.index(max(values.shape))
    next_to = place[:longest] + [(place[longest] + 1) % values.shape[longest]] + place[longest + 1:]
    return values.at[tuple(place)].set(smallest).at[tuple(next_to)].set(high)


def level_of(own_key, shape, cuts, low, top_value):
    def one(position, shards_of):
        draws = jax.random.uniform(jax.random.fold_in(jax.random.fold_in(own_key, 6), position), (shards_of,), jnp.float32, low / len(cuts), top_value / len(cuts))
        return jnp.repeat(jnp.exp(draws), shape[position] // shards_of).reshape((-1,) + (1,) * (len(shape) - position - 1))

    level = one(*cuts[0])
    for cut in cuts[1:]:
        level = level * one(*cut)
    return level


def scatter_about(key, shape, scale, limit, cuts=(), held_as=jnp.bfloat16):
    level = level_of(key, shape, cuts, -0.22, 0.18) if cuts else 1.0
    entries = jax.random.normal(key, shape, jnp.float32) * scale * level
    return jnp.minimum(jnp.maximum(entries, -limit), limit).astype(held_as)


def setup_inputs(seed: int = 0) -> dict:
    key_of = jax.random.split(jax.random.key(seed), 9)
    return {
        "wind": scatter_about(key_of[0], (SCENS, HOURS, BUSES), 0.5, 4.0, ((0, 16), (2, 16))),
        "load": jnp.clip(1.5 * jax.random.uniform(key_of[1], (HOURS, BUSES), jnp.float32) ** level_of(key_of[1], (HOURS, BUSES), ((1, 16),), -0.2, 0.2), 0.0, 1.5).astype(jnp.bfloat16),
        "ptdf_tiles": scatter_about(key_of[2], (LINES // TILE, NZ, TILE, TILE), (NZ * TILE) ** -0.5, 0.09375, ((0, 16),)),
        "tile_cols": draw_tile_cols(jax.random.fold_in(key_of[8], 71), 0),
        "line_cap": jnp.clip(jnp.exp(math.log(3.0) - 2.3025851 * jax.random.uniform(key_of[4], (LINES,), jnp.float32) ** level_of(key_of[4], (LINES,), ((0, 16),), -0.2, 0.2)), 0.3, 3.0),
        "gen_bus": draw_gen_bus(jax.random.fold_in(key_of[8], 71), 0),
        "gen_data": draw_gen_data(jax.random.fold_in(key_of[8], 71), 0),
        "prob_weight": touch_ends(jax.random.randint(key_of[7], (SCENS,), 1, 17), jax.random.fold_in(key_of[7], 1), 1, 16).astype(jnp.int32),
    }


penalty = 1.0
flow_weight = 0.25
commit_step = 0.5


def rounded(values):
    return lax.optimization_barrier(values.astype(jnp.bfloat16)).astype(jnp.float32)


def scenario_steps(state, load, ptdf_wide, tile_cols, line_cap, gen_bus, gen_data, comm_mean, disp_mean):
    dispatch, commit, w_disp, w_comm, wind_s = state
    linear, quadratic, fixed_cost, capacity = gen_data[0], gen_data[1], gen_data[2], gen_data[3]
    step_gen = 1.0 / (quadratic + penalty + 2.0)
    bus_tiles = BUSES // TILE
    line_tiles = LINES // TILE
    lt_dev = line_tiles // N_AREA
    flow = jnp.zeros((HOURS, LINES), jnp.float32)
    for step_index in range(STEPS):
        placed = jax.ops.segment_sum(dispatch.T, gen_bus, num_segments=BUSES).T
        injection = (placed + wind_s.astype(jnp.float32) - load.astype(jnp.float32)).astype(jnp.bfloat16)
        inj_f = injection.astype(jnp.float32)
        picked = inj_f.reshape(HOURS, bus_tiles, TILE)[:, tile_cols]
        flow = jnp.einsum("hkzb,kzlb->hkl", picked, ptdf_wide).reshape(HOURS, LINES)
        excess = flow - jnp.clip(flow, -line_cap, line_cap)
        imbalance = jnp.sum(inj_f, axis=1)
        ex_b = rounded(excess).reshape(HOURS, line_tiles, TILE)
        contrib = jnp.einsum("hkl,kzlb->hkzb", ex_b, ptdf_wide)
        contrib = contrib.reshape(HOURS, N_AREA, lt_dev, NZ, TILE)
        area_idx = jnp.arange(N_AREA, dtype=jnp.int32)[:, None, None]
        cols_r = tile_cols.reshape(N_AREA, lt_dev, NZ)
        partial_value = jnp.zeros((HOURS, N_AREA, bus_tiles, TILE), jnp.float32).at[:, area_idx, cols_r].add(contrib)
        price = jnp.sum(rounded(partial_value), axis=1).reshape(HOURS, BUSES)
        grad = linear + quadratic * dispatch + flow_weight * price[:, gen_bus] + imbalance[:, None] / BUSES + w_disp + penalty * (dispatch - disp_mean)
        commit = jnp.clip(commit - commit_step * (fixed_cost - dispatch / capacity + w_comm + penalty * (commit - comm_mean)), 0.0, 1.0)
        dispatch = jnp.clip(dispatch - step_gen * grad, 0.0, capacity * commit)
    return dispatch, commit, flow


def reference(wind, load, ptdf_tiles, tile_cols, line_cap, gen_bus, gen_data, prob_weight):
    weights = prob_weight.astype(jnp.float32)
    prob = weights / jnp.sum(weights)
    capacity = gen_data[3]
    ptdf_wide = ptdf_tiles.astype(jnp.float32)
    commit = jnp.full((SCENS, HOURS, GENS), 0.5, jnp.float32)
    dispatch = jnp.zeros((SCENS, HOURS, GENS), jnp.float32) + 0.25 * capacity
    comm_mean = jnp.full((HOURS, GENS), 0.5, jnp.float32)
    disp_mean = jnp.zeros((HOURS, GENS), jnp.float32) + 0.25 * capacity
    w_comm = jnp.zeros((SCENS, HOURS, GENS), jnp.float32)
    w_disp = jnp.zeros((SCENS, HOURS, GENS), jnp.float32)
    flows = jnp.zeros((SCENS, HOURS, LINES), jnp.float32)
    for round_index in range(ITERS):
        def one_scenario(state):
            return scenario_steps(state, load, ptdf_wide, tile_cols, line_cap, gen_bus, gen_data, comm_mean, disp_mean)
        dispatch, commit, flows = lax.map(one_scenario, (dispatch, commit, w_disp, w_comm, wind))
        comm_mean = jnp.sum(prob[:, None, None] * commit, axis=0)
        disp_mean = jnp.sum(prob[:, None, None] * dispatch, axis=0)
        w_comm = w_comm + penalty * (commit - comm_mean)
        w_disp = w_disp + penalty * (dispatch - disp_mean)
    return comm_mean, disp_mean, dispatch, flows
```

```python
import jax
import jax.numpy as jnp
from jax import lax
from jax.experimental import pallas as pl
from jax.experimental.pallas import tpu as pltpu
from jax.sharding import PartitionSpec as P

BUSES = 24576
penalty = 1.0
flow_weight = 0.25
commit_step = 0.5
F32 = jnp.float32
BF16 = jnp.bfloat16
MIB = 1 << 20


def nt(a, b):
    return lax.dot_general(a, b, (((1,), (1,)), ((), ())), preferred_element_type=F32)


def nn(a, b):
    return jnp.dot(a, b, preferred_element_type=F32)


def at_shared_buses(dispatch, same):
    high = dispatch.astype(BF16)
    rest = dispatch - high.astype(F32)
    middle = rest.astype(BF16)
    low = (rest - middle.astype(F32)).astype(BF16)
    return nn(high, same) + (nn(middle, same) + nn(low, same))


def gen_injection(dispatch, same, outside_gen, first):
    placed = at_shared_buses(dispatch, same)
    return jnp.where(first > 0.5, placed + outside_gen, 0.0).astype(BF16)


def prepare_kernel(wind, load, bus_col, bus_row, data, sent, same, outside_gen, first):
    rows, buses = wind.shape
    gens = bus_col.shape[0]
    col, row = bus_col[...], bus_row[...]
    onehot = (col == lax.broadcasted_iota(jnp.int32, (gens, buses), 1)).astype(F32).astype(BF16)
    held = nn(jnp.ones((8, gens), BF16), onehot)[:1]
    out_gen = nt(wind[...], onehot) - nt(load[...], onehot)
    outside_gen[...] = out_gen
    shared = col == row
    same_here = shared.astype(F32).astype(BF16)
    same[...] = same_here
    earlier = shared & (
        lax.broadcasted_iota(jnp.int32, (gens, gens), 0) < lax.broadcasted_iota(jnp.int32, (gens, gens), 1)
    )
    first_here = 1.0 - jnp.max(earlier.astype(F32), axis=0, keepdims=True)
    first[...] = first_here
    dispatch = jnp.broadcast_to(0.25 * data[3:4, :], (rows, gens))
    injection = gen_injection(dispatch, same_here, out_gen, first_here)
    base = jnp.where(held > 0.5, 0.0, wind[...].astype(F32) - load[...].astype(F32)).astype(BF16)
    tile_at = row // 128
    lane_at = (row - 128 * tile_at).astype(F32)
    tile_at = tile_at.astype(F32)
    line = lax.broadcasted_iota(jnp.int32, (rows, 128), 0)
    places = jnp.where(
        line == 0,
        tile_at[:, :128],
        jnp.where(
            line == 1,
            tile_at[:, 128:],
            jnp.where(line == 2, lane_at[:, :128], jnp.where(line == 3, lane_at[:, 128:], 0.0)),
        ),
    ).astype(BF16)
    for copy in range(sent.shape[0]):
        for j in range(12):
            sent[copy, j] = base[:, 128 * j : 128 * (j + 1)]
        sent[copy, 12] = injection[:, :128]
        sent[copy, 13] = injection[:, 128:]
        sent[copy, 14] = places


def flows_and_prices(inject, matrix, base, cap, flow, partial):
    areas, lines, _ = matrix.shape
    excess = []
    for b in range(lines // 256):
        rows = pl.ds(256 * b, 256)
        total = base[:, rows]
        for a in range(areas):
            total = total + nt(inject(a), matrix[a, rows, :])
        flow[:, rows] = total
        limit = cap[:, rows]
        excess.append((total - jnp.clip(total, -limit, limit)).astype(BF16))
    excess = jnp.concatenate(excess, axis=1)
    for a in range(areas):
        partial[a] = nn(excess, matrix[a]).astype(BF16)


def start_kernel(cols, core, tiles, mine, other, cap, matrix, partial, base, imb_base, imbalance, flow, held, code):
    k = pl.program_id(0)
    areas = matrix.shape[0]
    rows = held.shape[2]
    c = core[0]

    @pl.when(k == 0)
    def _():
        for chip in range(areas // 2):
            held[2 * chip + c] = mine[chip]
            held[2 * chip + 1 - c] = other[chip]
        total = jnp.zeros((rows, 128), F32)
        gen_total = jnp.zeros((rows, 128), F32)
        for a in range(areas):
            for j in range(12):
                total += held[a, j].astype(F32)
            for j in range(12, 14):
                gen_total += held[a, j].astype(F32)
            place = held[a, 14].astype(F32)
            code[a, :, :128] = place[0:1] * 128.0 + place[2:3]
            code[a, :, 128:] = place[1:2] * 128.0 + place[3:4]
        before = jnp.broadcast_to(jnp.sum(total, axis=1, keepdims=True), (rows, 128))
        imb_base[...] = before
        imbalance[...] = before + jnp.broadcast_to(jnp.sum(gen_total, axis=1, keepdims=True), (rows, 128))
        matrix[...] = jnp.zeros_like(matrix)

    at_bus = lax.broadcasted_iota(jnp.int32, (128, 256), 0).astype(F32)
    here = pl.ds(pl.multiple_of(k * 128, 128), 128)

    def slot(z, total):
        t = cols[k, z]
        a = t // 12
        j = t - 12 * a
        tile = tiles[0, z]
        total = total + nt(held[a, j], tile)
        bus = code[a] - (128 * j).astype(F32)
        pick = jnp.where(at_bus == bus, 1.0, 0.0).astype(BF16)
        matrix[a, here, :] = matrix[a, here, :] + nn(tile, pick).astype(BF16)
        return total

    total = lax.fori_loop(0, tiles.shape[1], slot, jnp.zeros((rows, 128), F32), unroll=4)
    base[:, here] = total

    @pl.when(k == pl.num_programs(0) - 1)
    def _():
        def inject(a):
            return jnp.concatenate([held[a, 12], held[a, 13]], axis=1)

        flows_and_prices(inject, matrix, base, cap, flow, partial)


def step_kernel(injection, matrix, base, imb_base, cap, partial, imbalance, flow):
    rows = injection.shape[1]
    flows_and_prices(lambda a: injection[a], matrix, base, cap, flow, partial)
    total = jnp.zeros((rows, injection.shape[2]), F32)
    for a in range(injection.shape[0]):
        total += injection[a].astype(F32)
    imbalance[...] = imb_base[...] + jnp.broadcast_to(jnp.sum(total, axis=1, keepdims=True), imbalance.shape)


def moved(data, prices, imbalance, commit, dispatch, w_comm, w_disp, comm_mean, disp_mean):
    linear, quadratic, fixed_cost, capacity = (data[i : i + 1, :] for i in range(4))
    price = prices[0].astype(F32)
    for a in range(1, prices.shape[0]):
        price = price + prices[a].astype(F32)
    grad = (
        linear
        + quadratic * dispatch
        + flow_weight * price
        + imbalance[:, :1] / BUSES
        + w_disp
        + penalty * (dispatch - disp_mean)
    )
    commit = jnp.clip(
        commit - commit_step * (fixed_cost - dispatch / capacity + w_comm + penalty * (commit - comm_mean)), 0.0, 1.0
    )
    step_gen = 1.0 / (quadratic + penalty + 2.0)
    return commit, jnp.clip(dispatch - step_gen * grad, 0.0, capacity * commit)


def send_injection(dispatch, same, outside_gen, first, sent):
    injection = gen_injection(dispatch, same[...], outside_gen[...], first[...])
    for copy in range(sent.shape[0]):
        sent[copy] = injection


def send_terms(weight, commit, dispatch, terms):
    rows = commit.shape[0]
    for copy in range(terms.shape[0]):
        terms[copy, :rows] = weight * commit
        terms[copy, rows : 2 * rows] = weight * dispatch


def first_update(prices, imbalance, data, same, outside_gen, first, commit_out, dispatch_out, sent):
    start = jnp.broadcast_to(0.25 * data[3:4, :], dispatch_out.shape)
    half = jnp.full(start.shape, 0.5, F32)
    commit, dispatch = moved(data, prices, imbalance, half, start, 0.0, 0.0, half, start)
    commit_out[...] = commit
    dispatch_out[...] = dispatch
    send_injection(dispatch, same, outside_gen, first, sent)


def second_update(
    prices, imbalance, data, same, outside_gen, first, commit_in, dispatch_in, weight,
    commit_out, dispatch_out, sent, terms,
):
    start = jnp.broadcast_to(0.25 * data[3:4, :], dispatch_out.shape)
    half = jnp.full(start.shape, 0.5, F32)
    commit, dispatch = moved(data, prices, imbalance, commit_in[...], dispatch_in[...], 0.0, 0.0, half, start)
    commit_out[...] = commit
    dispatch_out[...] = dispatch
    send_injection(dispatch, same, outside_gen, first, sent)
    send_terms(weight[...], commit, dispatch, terms)
    for copy in range(terms.shape[0]):
        terms[copy, 48:] = jnp.broadcast_to(weight[...], (8, commit.shape[1]))


def means_of(terms):
    rows = (terms.shape[1] - 8) // 2
    total = terms[0]
    for s in range(1, terms.shape[0]):
        total = total + terms[s]
    weights = total[2 * rows : 2 * rows + 1]
    return total[:rows] / weights, total[rows : 2 * rows] / weights, weights


def third_update(
    prices, imbalance, data, same, outside_gen, first, commit_in, dispatch_in, terms,
    commit_out, dispatch_out, sent, kept,
):
    comm_mean, disp_mean, weights = means_of(terms)
    commit, dispatch = commit_in[...], dispatch_in[...]
    w_comm = penalty * (commit - comm_mean)
    w_disp = penalty * (dispatch - disp_mean)
    kept[0] = w_comm
    kept[1] = w_disp
    kept[2] = comm_mean
    kept[3] = disp_mean
    kept[4] = jnp.broadcast_to(weights, commit.shape)
    commit, dispatch = moved(data, prices, imbalance, commit, dispatch, w_comm, w_disp, comm_mean, disp_mean)
    commit_out[...] = commit
    dispatch_out[...] = dispatch
    send_injection(dispatch, same, outside_gen, first, sent)


def last_update(prices, imbalance, data, commit_in, dispatch_in, weight, kept, dispatch_out, terms):
    commit, dispatch = moved(
        data, prices, imbalance, commit_in[...], dispatch_in[...], kept[0], kept[1], kept[2], kept[3]
    )
    dispatch_out[...] = dispatch
    send_terms(weight[...], commit, dispatch, terms)


def last_means(terms, kept, comm_mean, disp_mean):
    rows = comm_mean.shape[0]
    total = terms[0]
    for s in range(1, terms.shape[0]):
        total = total + terms[s]
    comm_mean[...] = total[:rows] / kept[4]
    disp_mean[...] = total[rows:] / kept[4]


def call(kernel, outs, *args, mib=24, **more):
    return pl.pallas_call(
        kernel,
        out_shape=[jax.ShapeDtypeStruct(shape, dtype) for shape, dtype in outs],
        compiler_params=pltpu.CompilerParams(vmem_limit_bytes=mib * MIB),
        **more,
    )(*args)


def spread(copies, axis):
    return lax.all_to_all(copies, axis, split_axis=0, concat_axis=0, tiled=True)


def on_device(wind, load, ptdf_tiles, tile_cols, line_cap, gen_bus, gen_data, prob_weight):
    _, hours, buses = wind.shape
    gens = gen_bus.shape[0]
    lines = line_cap.shape[0]
    areas = lax.axis_size("area")
    scens = lax.axis_size("scen")
    area = lax.axis_index("area")
    core = area % 2
    local = gen_bus - area * buses
    cap = line_cap[None, :]
    weight = jnp.broadcast_to(prob_weight.astype(F32)[:, None], (1, gens))

    sent, same, outside_gen, first = call(
        prepare_kernel,
        [((areas // 2, 15, hours, 128), BF16), ((gens, gens), BF16), ((hours, gens), F32), ((1, gens), F32)],
        wind[0], load, local[:, None], local[None, :], gen_data,
    )
    chips = [[2 * i + c for i in range(areas // 2)] for c in range(2)]
    mine = lax.all_to_all(sent, "area", split_axis=0, concat_axis=0, tiled=True, axis_index_groups=chips)
    other = lax.ppermute(mine, "area", [(i, i ^ 1) for i in range(areas)])

    def whole(shape):
        return pl.BlockSpec(shape, lambda k: (0,) * len(shape))

    state = (hours, gens)
    matrix, partial, base, imb_base, imbalance, flow = call(
        start_kernel,
        [
            ((areas, lines, gens), BF16),
            ((areas, hours, gens), BF16),
            ((hours, lines), F32),
            ((hours, 128), F32),
            ((hours, 128), F32),
            ((hours, lines), F32),
        ],
        tile_cols, core[None], ptdf_tiles, mine, other, cap,
        mib=40,
        grid=(ptdf_tiles.shape[0],),
        in_specs=[
            pl.BlockSpec(memory_space=pltpu.SMEM),
            pl.BlockSpec(memory_space=pltpu.SMEM),
            pl.BlockSpec((1, *ptdf_tiles.shape[1:]), lambda k: (k, 0, 0, 0)),
            whole(mine.shape),
            whole(other.shape),
            whole(cap.shape),
        ],
        out_specs=[
            whole((areas, lines, gens)),
            whole((areas, hours, gens)),
            whole((hours, lines)),
            whole((hours, 128)),
            whole((hours, 128)),
            whole((hours, lines)),
        ],
        scratch_shapes=[pltpu.VMEM((areas, 15, hours, 128), BF16), pltpu.VMEM((areas, 1, gens), F32)],
    )

    def step(injection):
        return call(
            step_kernel,
            [((areas, hours, gens), BF16), ((hours, 128), F32), ((hours, lines), F32)],
            injection, matrix, base, imb_base, cap,
        )

    local_args = (gen_data, same, outside_gen, first)
    stated = [(state, F32), (state, F32), ((areas, *state), BF16)]
    commit, dispatch, sent = call(first_update, stated, spread(partial, "area"), imbalance, *local_args)
    partial, imbalance, _ = step(spread(sent, "area"))
    commit, dispatch, sent, terms = call(
        second_update,
        [*stated, ((scens, 2 * hours + 8, gens), F32)],
        spread(partial, "area"), imbalance, *local_args, commit, dispatch, weight,
    )
    terms = spread(terms, "scen")
    partial, imbalance, _ = step(spread(sent, "area"))
    commit, dispatch, sent, kept = call(
        third_update,
        [*stated, ((5, *state), F32)],
        spread(partial, "area"), imbalance, *local_args, commit, dispatch, terms,
    )
    partial, imbalance, flow = step(spread(sent, "area"))
    dispatch, terms = call(
        last_update,
        [(state, F32), ((scens, 2 * hours, gens), F32)],
        spread(partial, "area"), imbalance, gen_data, commit, dispatch, weight, kept,
    )
    comm_mean, disp_mean = call(last_means, [(state, F32), (state, F32)], spread(terms, "scen"), kept)
    return comm_mean, disp_mean, dispatch[None], flow[None]


def solution(mesh):
    placed = (
        P("scen", None, "area"),
        P(None, "area"),
        P("area", None, None, None),
        P("area", None),
        P("area"),
        P("area"),
        P(None, "area"),
        P("scen"),
    )
    return jax.shard_map(
        on_device,
        mesh=mesh,
        in_specs=placed,
        out_specs=(
            P(None, "area"),
            P(None, "area"),
            P("scen", None, "area"),
            P("scen", None, "area"),
        ),
        check_vma=False,
    )
```

```python
import jax
import jax.numpy as jnp
from jax import lax
from jax.experimental import pallas as pl
from jax.experimental.pallas import tpu as pltpu
from jax.sharding import PartitionSpec as P

BUSES = 24576
penalty = 1.0
flow_weight = 0.25
commit_step = 0.5
F32 = jnp.float32
BF16 = jnp.bfloat16
MIB = 1 << 20


def nt(a, b):
    return lax.dot_general(a, b, (((1,), (1,)), ((), ())), preferred_element_type=F32)


def nn(a, b):
    return jnp.dot(a, b, preferred_element_type=F32)


def at_shared_buses(dispatch, same):
    high = dispatch.astype(BF16)
    rest = dispatch - high.astype(F32)
    middle = rest.astype(BF16)
    low = (rest - middle.astype(F32)).astype(BF16)
    return nn(high, same) + (nn(middle, same) + nn(low, same))


def gen_injection(dispatch, same, outside_gen, first):
    placed = at_shared_buses(dispatch, same)
    return jnp.where(first > 0.5, placed + outside_gen, 0.0).astype(BF16)


def first_of(shared):
    gens = shared.shape[0]
    earlier = shared & (
        lax.broadcasted_iota(jnp.int32, (gens, gens), 0) < lax.broadcasted_iota(jnp.int32, (gens, gens), 1)
    )
    return 1.0 - jnp.max(earlier.astype(F32), axis=0, keepdims=True)


def as_column(row):
    return jnp.transpose(jnp.broadcast_to(row, (128, row.shape[1])))[:, :1]


def pieces_of(values):
    high = values.astype(BF16).astype(F32)
    middle = (values - high).astype(BF16).astype(F32)
    return high, middle, values - high - middle


def stacked(lines, rows):
    line = lax.broadcasted_iota(jnp.int32, (rows, lines[0].shape[1]), 0)
    out = jnp.zeros(line.shape, F32)
    for i, values in enumerate(lines):
        out = jnp.where(line == i, values, out)
    return out.astype(BF16)


def prepare_kernel(area, wind, load, bus, data, sent):
    rows, buses = wind.shape
    gens = bus.shape[1]
    row_int = bus[...] - area[0] * buses
    row = row_int.astype(F32)
    col = as_column(row)
    onehot = (col == lax.broadcasted_iota(jnp.int32, (gens, buses), 1).astype(F32)).astype(F32).astype(BF16)
    held = nn(jnp.ones((8, gens), BF16), onehot)[:1]
    wind_gen, load_gen = nt(wind[...], onehot), nt(load[...], onehot)
    shared = col == row
    dispatch = jnp.broadcast_to(0.25 * data[3:4, :], (rows, gens))
    injection = gen_injection(dispatch, shared.astype(F32).astype(BF16), wind_gen - load_gen, first_of(shared))
    base = jnp.where(held > 0.5, 0.0, wind[...].astype(F32) - load[...].astype(F32)).astype(BF16)
    tile_at = row_int // 128
    lane_at = (row_int - 128 * tile_at).astype(F32)
    lines = [tile_at.astype(F32), lane_at]
    for i in range(4):
        lines.extend(pieces_of(data[i : i + 1, :]))
    wind_gen, load_gen = wind_gen.astype(BF16), load_gen.astype(BF16)
    for half in range(2):
        lanes = slice(128 * half, 128 * (half + 1))
        info = stacked([values[:, lanes] for values in lines], rows)
        for copy in range(sent.shape[0]):
            sent[copy, 12 + half] = injection[:, lanes]
            sent[copy, 14 + half] = info
            sent[copy, 16 + half] = wind_gen[:, lanes]
            sent[copy, 18 + half] = load_gen[:, lanes]
    for copy in range(sent.shape[0]):
        for j in range(12):
            sent[copy, j] = base[:, 128 * j : 128 * (j + 1)]


def side_by_side(blocks, *at):
    left, right = blocks[at].astype(F32), blocks[(*at[:-1], at[-1] + 1)].astype(F32)
    return jnp.concatenate([left, right], axis=1)


def params_kernel(prob_weight, mine, cols, cap, data, same, outside_gen, first, weight, cols_out, cap_out):
    cols_out[...] = cols[...]
    cap_out[...] = cap[...]
    weight[...] = jnp.full(weight.shape, prob_weight[0].astype(F32))
    for chip in range(mine.shape[0]):
        info = side_by_side(mine, chip, 14)
        bus = info[0:1] * 128.0 + info[1:2]
        shared = as_column(bus) == bus
        same[chip] = shared.astype(F32).astype(BF16)
        first[chip] = first_of(shared)
        for i in range(4):
            at = 2 + 3 * i
            data[chip, i : i + 1] = info[at : at + 1] + info[at + 1 : at + 2] + info[at + 2 : at + 3]
        outside_gen[chip] = side_by_side(mine, chip, 16) - side_by_side(mine, chip, 18)


def add_flow(total, inject, matrix, area, rows):
    return total + nt(inject, matrix[area, rows, :])


def excess_of(flow, limit):
    return (flow - jnp.clip(flow, -limit, limit)).astype(BF16)


def lane_sum(total):
    return jnp.broadcast_to(jnp.sum(total, axis=1, keepdims=True), (total.shape[0], 128))


def start_kernel(
    cols, area, tiles, mine, other, cap,
    matrix, partial, base, imb_base, imbalance, excess, held, code,
):
    k = pl.program_id(0)
    areas = matrix.shape[0]
    rows = held.shape[2]
    c = lax.rem(area[0], 2)

    @pl.when(k == 0)
    def _():
        for chip in range(areas // 2):
            for j in range(16):
                held[2 * chip + c, j] = mine[chip, j]
                held[2 * chip + 1 - c, j] = other[chip, j]
        total = jnp.zeros((rows, 128), F32)
        gen_total = jnp.zeros((rows, 128), F32)
        for a in range(areas):
            for j in range(12):
                total += held[a, j].astype(F32)
            for j in range(12, 14):
                gen_total += held[a, j].astype(F32)
            info = side_by_side(held, a, 14)
            code[a] = info[0:1] * 128.0 + info[1:2]
        before = lane_sum(total)
        imb_base[...] = before
        imbalance[...] = before + lane_sum(gen_total)
        matrix[...] = jnp.zeros_like(matrix)

    at_bus = lax.broadcasted_iota(jnp.int32, (128, 256), 0).astype(F32)
    here = pl.ds(pl.multiple_of(k * 128, 128), 128)

    total = jnp.zeros((rows, 128), F32)
    for z in range(tiles.shape[1]):
        t = cols[k, z]
        a = t // 12
        j = t - 12 * a
        tile = tiles[0, z]
        total = total + nt(held[a, j], tile)
        bus = code[a] - (128 * j).astype(F32)
        pick = jnp.where(at_bus == bus, 1.0, 0.0).astype(BF16)
        matrix[a, here, :] = matrix[a, here, :] + nn(tile, pick).astype(BF16)
    base[:, here] = total

    @pl.when(k == pl.num_programs(0) - 1)
    def _():
        over = []
        for b in range(matrix.shape[1] // 256):
            lines = pl.ds(256 * b, 256)
            flow = base[:, lines]
            for a in range(areas):
                inject = jnp.concatenate([held[a, 12], held[a, 13]], axis=1)
                flow = add_flow(flow, inject, matrix, a, lines)
            over.append(excess_of(flow, cap[:, lines]))
        over = jnp.concatenate(over, axis=1)
        excess[...] = over
        for chip in range(areas // 2):
            partial[chip] = nn(over, matrix[2 * chip + 1 - c]).astype(BF16)


def own_side_prices(area, excess, matrix, partial):
    c = lax.rem(area[0], 2)
    for chip in range(partial.shape[0]):
        partial[chip] = nn(excess[...], matrix[2 * chip + c])


def both_sides(mine, other, sent):
    for chip in range(mine.shape[0]):
        total = (mine[chip] + other[chip].astype(F32)).astype(BF16)
        for copy in range(sent.shape[0]):
            sent[copy, chip] = total


def own_side_flow(area, injection, matrix, base, flow):
    c = lax.rem(area[0], 2)
    for b in range(matrix.shape[1] // 256):
        lines = pl.ds(256 * b, 256)
        total = base[:, lines]
        for chip in range(injection.shape[0]):
            total = add_flow(total, injection[chip], matrix, 2 * chip + c, lines)
        flow[:, lines] = total


def other_side_flow(area, half_flow, mine, other, matrix, imb_base, cap, partial, imbalance, excess):
    c = lax.rem(area[0], 2)
    chips = mine.shape[0]
    over = []
    for b in range(matrix.shape[1] // 256):
        lines = pl.ds(256 * b, 256)
        total = half_flow[:, lines]
        for chip in range(chips):
            total = add_flow(total, other[chip], matrix, 2 * chip + 1 - c, lines)
        over.append(excess_of(total, cap[:, lines]))
    over = jnp.concatenate(over, axis=1)
    excess[...] = over
    if partial.shape[0] == chips:
        for chip in range(chips):
            partial[chip] = nn(over, matrix[2 * chip + 1 - c]).astype(BF16)
    else:
        for a in range(2 * chips):
            partial[a] = nn(over, matrix[a]).astype(BF16)
    total = jnp.zeros(mine.shape[1:], F32)
    for chip in range(chips):
        total += mine[chip].astype(F32) + other[chip].astype(F32)
    imbalance[...] = imb_base[...] + lane_sum(total)


def step_kernel(injection, matrix, base, imb_base, cap, partial, imbalance, flow):
    areas, lines, _ = matrix.shape
    over = []
    for b in range(lines // 256):
        rows = pl.ds(256 * b, 256)
        total = base[:, rows]
        for a in range(areas):
            total = add_flow(total, injection[a], matrix, a, rows)
        flow[:, rows] = total
        over.append(excess_of(total, cap[:, rows]))
    over = jnp.concatenate(over, axis=1)
    for a in range(areas):
        partial[a] = nn(over, matrix[a]).astype(BF16)
    total = jnp.zeros(injection.shape[1:], F32)
    for a in range(areas):
        total += injection[a].astype(F32)
    imbalance[...] = imb_base[...] + lane_sum(total)


def moved(data, price, imbalance, commit, dispatch, w_comm, w_disp, comm_mean, disp_mean):
    linear, quadratic, fixed_cost, capacity = (data[i : i + 1] for i in range(4))
    grad = (
        linear
        + quadratic * dispatch
        + flow_weight * price
        + imbalance[:, :1] / BUSES
        + w_disp
        + penalty * (dispatch - disp_mean)
    )
    commit = jnp.clip(
        commit - commit_step * (fixed_cost - dispatch / capacity + w_comm + penalty * (commit - comm_mean)), 0.0, 1.0
    )
    step_gen = 1.0 / (quadratic + penalty + 2.0)
    return commit, jnp.clip(dispatch - step_gen * grad, 0.0, capacity * commit)


def summed(prices, at):
    total = prices[(0, *at)].astype(F32)
    for i in range(1, prices.shape[0]):
        total = total + prices[(i, *at)].astype(F32)
    return total


def first_update(prices, imbalance, data, same, outside_gen, first, commit_out, dispatch_out, injection):
    shape = dispatch_out.shape[1:]
    for chip in range(data.shape[0]):
        values = data[chip]
        start = jnp.broadcast_to(0.25 * values[3:4], shape)
        half = jnp.full(shape, 0.5, F32)
        commit, dispatch = moved(values, summed(prices, (chip,)), imbalance, half, start, 0.0, 0.0, half, start)
        commit_out[chip] = commit
        dispatch_out[chip] = dispatch
        injection[chip] = gen_injection(dispatch, same[chip], outside_gen[chip], first[chip])


def second_update(
    area, prices, imbalance, data, same, outside_gen, first, commit_in, dispatch_in, weight,
    state_out, injection, terms, kept,
):
    shape = dispatch_in.shape[1:]
    for chip in range(data.shape[0]):
        values = data[chip]
        start = jnp.broadcast_to(0.25 * values[3:4], shape)
        half = jnp.full(shape, 0.5, F32)
        commit, dispatch = moved(
            values, summed(prices, (chip,)), imbalance, commit_in[chip], dispatch_in[chip], 0.0, 0.0, half, start
        )
        injection[chip] = gen_injection(dispatch, same[chip], outside_gen[chip], first[chip])
        kept[0, chip] = commit
        kept[1, chip] = dispatch
    for i in range(2):
        value = kept[i, lax.div(area[0], 2)]
        state_out[i] = value
        terms[i] = weight[:1] * value
    terms[2] = jnp.broadcast_to(weight[:1], shape)


def add_terms(*refs):
    refs[-1][...] = (refs[0][...] + refs[1][...]) + (refs[2][...] + refs[3][...])


def third_update(
    area, prices, imbalance, data, same, outside_gen, first, state, weight, terms0, terms1, terms2, terms3,
    state_out, sent, means, prob,
):
    commit, dispatch = state[0], state[1]
    total = [(terms0[i] + terms1[i]) + (terms2[i] + terms3[i]) for i in range(3)]
    comm_mean, disp_mean = total[0] / total[2], total[1] / total[2]
    prob[...] = weight[...] / total[2][:8]
    w_comm = penalty * (commit - comm_mean)
    w_disp = penalty * (dispatch - disp_mean)
    means[0] = comm_mean
    means[1] = disp_mean
    me = lax.div(area[0], 2)
    commit, dispatch = moved(
        data[me], summed(prices, ()), imbalance, commit, dispatch, w_comm, w_disp, comm_mean, disp_mean
    )
    state_out[0] = commit
    state_out[1] = dispatch
    state_out[2] = w_comm
    state_out[3] = w_disp
    injection = gen_injection(dispatch, same[me], outside_gen[me], first[me])
    for copy in range(sent.shape[0]):
        sent[copy] = injection


def last_update(area, prices, imbalance, data, state, means, prob, dispatch_out, terms):
    commit, dispatch = moved(
        data[lax.div(area[0], 2)], summed(prices, ()), imbalance, state[0], state[1], state[2], state[3], means[0], means[1]
    )
    dispatch_out[...] = dispatch
    share = prob[:1]
    commit = (share * (commit - means[0])).astype(BF16)
    dispatch = (share * (dispatch - means[1])).astype(BF16)
    for copy in range(terms.shape[0]):
        terms[copy, 0] = commit
        terms[copy, 1] = dispatch


def last_means(terms, means, comm_mean, disp_mean):
    comm_mean[...] = means[0] + summed(terms, (0,))
    disp_mean[...] = means[1] + summed(terms, (1,))


def call(kernel, outs, *args, mib=4, cost=1, scalars=0, **more):
    if scalars:
        memories = [pltpu.SMEM] * scalars + [pltpu.VMEM] * (len(args) - scalars)
        more["in_specs"] = [pl.BlockSpec(memory_space=memory) for memory in memories]
    return pl.pallas_call(
        kernel,
        out_shape=[jax.ShapeDtypeStruct(shape, dtype) for shape, dtype in outs],
        compiler_params=pltpu.CompilerParams(vmem_limit_bytes=mib * MIB),
        cost_estimate=pl.CostEstimate(flops=0, transcendentals=0, bytes_accessed=cost * 3_000_000),
        **more,
    )(*args)


def spread(copies, axis, groups=None):
    return lax.all_to_all(copies, axis, split_axis=0, concat_axis=0, tiled=True, axis_index_groups=groups)


def swapped(block, axis, bits):
    return lax.ppermute(block, axis, [(i, i ^ bits) for i in range(lax.axis_size(axis))])


def on_device(wind, load, ptdf_tiles, tile_cols, line_cap, gen_bus, gen_data, prob_weight):
    _, hours, buses = wind.shape
    gens = gen_bus.shape[0]
    lines = line_cap.shape[0]
    areas = lax.axis_size("area")
    scens = lax.axis_size("scen")
    chips = areas // 2
    area = lax.axis_index("area")[None]
    groups = [[2 * i + c for i in range(chips)] for c in range(2)]
    state = (hours, gens)

    [sent] = call(
        prepare_kernel,
        [((chips, 20, hours, 128), BF16)],
        area, wind[0], load, gen_bus[None, :], gen_data,
        mib=56, scalars=1,
    )
    mine = spread(sent, "area", groups)
    other = swapped(mine, "area", 1)
    *params, weight, cols, cap = call(
        params_kernel,
        [
            ((chips, 4, gens), F32),
            ((chips, gens, gens), BF16),
            ((chips, *state), F32),
            ((chips, 1, gens), F32),
            ((8, gens), F32),
            (tile_cols.shape, jnp.int32),
            ((1, lines), F32),
        ],
        prob_weight, mine, tile_cols, line_cap[None, :],
        mib=8, scalars=1,
    )

    def whole(shape):
        return pl.BlockSpec(shape, lambda k: (0,) * len(shape))

    starts = [
        ((areas, lines, gens), BF16),
        ((chips, *state), BF16),
        ((hours, lines), F32),
        ((hours, 128), F32),
        ((hours, 128), F32),
        ((hours, lines), BF16),
    ]
    matrix, partial, base, imb_base, imbalance, excess = call(
        start_kernel,
        starts,
        cols, area, ptdf_tiles, mine, other, cap,
        mib=40, cost=16,
        grid=(ptdf_tiles.shape[0],),
        in_specs=[
            pl.BlockSpec(memory_space=pltpu.SMEM),
            pl.BlockSpec(memory_space=pltpu.SMEM),
            pl.BlockSpec((1, *ptdf_tiles.shape[1:]), lambda k: (k, 0, 0, 0)),
            whole(mine.shape),
            whole(other.shape),
            whole(cap.shape),
        ],
        out_specs=[whole(shape) for shape, _ in starts],
        scratch_shapes=[pltpu.VMEM((areas, 16, hours, 128), BF16), pltpu.VMEM((areas, 1, gens), F32)],
    )

    def all_prices(partial, excess):
        theirs = swapped(partial, "area", 1)
        [ours] = call(own_side_prices, [((chips, *state), F32)], area, excess, matrix, cost=2, scalars=1)
        [sent] = call(both_sides, [((chips, chips, *state), BF16)], ours, theirs)
        return spread(sent, "area", groups)

    def flow_and_prices(injection, count):
        theirs = swapped(injection, "area", 1)
        [half] = call(own_side_flow, [((hours, lines), F32)], area, injection, matrix, base, cost=2, scalars=1)
        return call(
            other_side_flow,
            [((count, *state), BF16), ((hours, 128), F32), ((hours, lines), BF16)],
            area, half, injection, theirs, matrix, imb_base, cap,
            cost=3, scalars=1,
        )

    eight = ((chips, *state), F32)
    commit, dispatch, injection = call(
        first_update,
        [eight, eight, ((chips, *state), BF16)],
        all_prices(partial, excess), imbalance, *params,
        mib=8,
    )
    partial, imbalance, excess = flow_and_prices(injection, chips)
    kept, injection, terms = call(
        second_update,
        [((2, *state), F32), ((chips, *state), BF16), ((3, *state), F32)],
        area, all_prices(partial, excess), imbalance, *params, commit, dispatch, weight,
        mib=8, scalars=1,
        scratch_shapes=[pltpu.VMEM((2, chips, *state), F32)],
    )
    near = [terms] + [swapped(terms, "scen", bits) for bits in (scens // 2, 1, scens // 2 + 1)]
    partial, imbalance, _ = flow_and_prices(injection, areas)
    [terms] = call(add_terms, [((3, *state), F32)], *near)
    far = [terms] + [swapped(terms, "scen", bits) for bits in (2, 4, 6)]
    partial, *far = lax.optimization_barrier((partial, *far))
    kept, sent, means, prob = call(
        third_update,
        [((4, *state), F32), ((areas, *state), BF16), ((2, *state), F32), ((8, gens), F32)],
        area, spread(partial, "area"), imbalance, *params, kept, weight, *far,
        scalars=1,
    )
    partial, imbalance, flow = call(
        step_kernel,
        [((areas, *state), BF16), ((hours, 128), F32), ((hours, lines), F32)],
        spread(sent, "area"), matrix, base, imb_base, cap,
        mib=6, cost=5,
    )
    dispatch, terms = call(
        last_update,
        [(state, F32), ((scens, 2, *state), BF16)],
        area, spread(partial, "area"), imbalance, params[0], kept, means, prob,
        scalars=1,
    )
    comm_mean, disp_mean = call(last_means, [(state, F32), (state, F32)], spread(terms, "scen"), means)
    return comm_mean, disp_mean, dispatch[None], flow[None]


def solution(mesh):
    placed = (
        P("scen", None, "area"),
        P(None, "area"),
        P("area", None, None, None),
        P("area", None),
        P("area"),
        P("area"),
        P(None, "area"),
        P("scen"),
    )
    return jax.shard_map(
        on_device,
        mesh=mesh,
        in_specs=placed,
        out_specs=(
            P(None, "area"),
            P(None, "area"),
            P("scen", None, "area"),
            P("scen", None, "area"),
        ),
        check_vma=False,
    )
```

```python
import jax
import jax.numpy as jnp
from jax import lax
from jax.experimental import pallas as pl
from jax.experimental.pallas import tpu as pltpu
from jax.sharding import PartitionSpec as P

BUSES = 24576
penalty = 1.0
flow_weight = 0.25
commit_step = 0.5
F32 = jnp.float32
BF16 = jnp.bfloat16
MIB = 1 << 20


def nt(a, b):
    return lax.dot_general(a, b, (((1,), (1,)), ((), ())), preferred_element_type=F32)


def nn(a, b):
    return jnp.dot(a, b, preferred_element_type=F32)


def at_shared_buses(dispatch, same):
    high = dispatch.astype(BF16)
    rest = dispatch - high.astype(F32)
    middle = rest.astype(BF16)
    low = (rest - middle.astype(F32)).astype(BF16)
    return nn(high, same) + (nn(middle, same) + nn(low, same))


def gen_injection(dispatch, same, outside_gen, first):
    placed = at_shared_buses(dispatch, same)
    return jnp.where(first > 0.5, placed + outside_gen, 0.0).astype(BF16)


def first_of(shared):
    gens = shared.shape[0]
    earlier = shared & (
        lax.broadcasted_iota(jnp.int32, (gens, gens), 0) < lax.broadcasted_iota(jnp.int32, (gens, gens), 1)
    )
    return 1.0 - jnp.max(earlier.astype(F32), axis=0, keepdims=True)


def as_column(row):
    return jnp.transpose(jnp.broadcast_to(row, (128, row.shape[1])))[:, :1]


def pieces_of(values):
    high = values.astype(BF16).astype(F32)
    middle = (values - high).astype(BF16).astype(F32)
    return high, middle, values - high - middle


def stacked(lines, rows):
    line = lax.broadcasted_iota(jnp.int32, (rows, lines[0].shape[1]), 0)
    out = jnp.zeros(line.shape, F32)
    for i, values in enumerate(lines):
        out = jnp.where(line == i, values, out)
    return out.astype(BF16)


def prepare_kernel(area, wind, load, bus, data, sent):
    rows, buses = wind.shape
    gens = bus.shape[1]
    row_int = bus[...] - area[0] * buses
    row = row_int.astype(F32)
    col = as_column(row)
    onehot = (col == lax.broadcasted_iota(jnp.int32, (gens, buses), 1).astype(F32)).astype(F32).astype(BF16)
    held = nn(jnp.ones((8, gens), BF16), onehot)[:1]
    wind_gen, load_gen = nt(wind[...], onehot), nt(load[...], onehot)
    shared = col == row
    dispatch = jnp.broadcast_to(0.25 * data[3:4, :], (rows, gens))
    injection = gen_injection(dispatch, shared.astype(F32).astype(BF16), wind_gen - load_gen, first_of(shared))
    base = jnp.where(held > 0.5, 0.0, wind[...].astype(F32) - load[...].astype(F32)).astype(BF16)
    tile_at = row_int // 128
    lane_at = (row_int - 128 * tile_at).astype(F32)
    lines = [tile_at.astype(F32), lane_at]
    for i in range(4):
        lines.extend(pieces_of(data[i : i + 1, :]))
    wind_gen, load_gen = wind_gen.astype(BF16), load_gen.astype(BF16)
    for half in range(2):
        lanes = slice(128 * half, 128 * (half + 1))
        info = stacked([values[:, lanes] for values in lines], rows)
        for copy in range(sent.shape[0]):
            sent[copy, 12 + half] = injection[:, lanes]
            sent[copy, 14 + half] = info
            sent[copy, 16 + half] = wind_gen[:, lanes]
            sent[copy, 18 + half] = load_gen[:, lanes]
    for copy in range(sent.shape[0]):
        for j in range(12):
            sent[copy, j] = base[:, 128 * j : 128 * (j + 1)]


def side_by_side(blocks, *at):
    left, right = blocks[at].astype(F32), blocks[(*at[:-1], at[-1] + 1)].astype(F32)
    return jnp.concatenate([left, right], axis=1)


def params_kernel(prob_weight, mine, cols, cap, data, same, outside_gen, first, weight, cols_out, cap_out):
    cols_out[...] = cols[...]
    cap_out[...] = cap[...]
    weight[...] = jnp.full(weight.shape, prob_weight[0].astype(F32))
    for chip in range(mine.shape[0]):
        info = side_by_side(mine, chip, 14)
        bus = info[0:1] * 128.0 + info[1:2]
        shared = as_column(bus) == bus
        same[chip] = shared.astype(F32).astype(BF16)
        first[chip] = first_of(shared)
        for i in range(4):
            at = 2 + 3 * i
            data[chip, i : i + 1] = info[at : at + 1] + info[at + 1 : at + 2] + info[at + 2 : at + 3]
        outside_gen[chip] = side_by_side(mine, chip, 16) - side_by_side(mine, chip, 18)


def add_flow(total, inject, matrix, area, rows):
    return total + nt(inject, matrix[area, rows, :])


def excess_of(flow, limit):
    return (flow - jnp.clip(flow, -limit, limit)).astype(BF16)


def lane_sum(total):
    return jnp.broadcast_to(jnp.sum(total, axis=1, keepdims=True), (total.shape[0], 128))


def start_kernel(
    cols, area, tiles, mine, other, cap,
    matrix, partial, base, imb_base, imbalance, excess, held, code,
):
    k = pl.program_id(0)
    areas = matrix.shape[0]
    rows = held.shape[2]
    c = lax.rem(area[0], 2)

    @pl.when(k == 0)
    def _():
        for chip in range(areas // 2):
            for j in range(16):
                held[2 * chip + c, j] = mine[chip, j]
                held[2 * chip + 1 - c, j] = other[chip, j]
        total = jnp.zeros((rows, 128), F32)
        gen_total = jnp.zeros((rows, 128), F32)
        for a in range(areas):
            for j in range(12):
                total += held[a, j].astype(F32)
            for j in range(12, 14):
                gen_total += held[a, j].astype(F32)
            info = side_by_side(held, a, 14)
            code[a] = info[0:1] * 128.0 + info[1:2]
        before = lane_sum(total)
        imb_base[...] = before
        imbalance[...] = before + lane_sum(gen_total)
        matrix[...] = jnp.zeros_like(matrix)

    at_bus = lax.broadcasted_iota(jnp.int32, (128, 256), 0).astype(F32)
    here = pl.ds(pl.multiple_of(k * 128, 128), 128)

    total = jnp.zeros((rows, 128), F32)
    for z in range(tiles.shape[1]):
        t = cols[k, z]
        a = t // 12
        j = t - 12 * a
        tile = tiles[0, z]
        total = total + nt(held[a, j], tile)
        bus = code[a] - (128 * j).astype(F32)
        pick = jnp.where(at_bus == bus, 1.0, 0.0).astype(BF16)
        matrix[a, here, :] = matrix[a, here, :] + nn(tile, pick).astype(BF16)
    base[:, here] = total

    @pl.when(k == pl.num_programs(0) - 1)
    def _():
        over = []
        for b in range(matrix.shape[1] // 256):
            lines = pl.ds(256 * b, 256)
            flow = base[:, lines]
            for a in range(areas):
                inject = jnp.concatenate([held[a, 12], held[a, 13]], axis=1)
                flow = add_flow(flow, inject, matrix, a, lines)
            over.append(excess_of(flow, cap[:, lines]))
        over = jnp.concatenate(over, axis=1)
        excess[...] = over
        for chip in range(areas // 2):
            partial[chip] = nn(over, matrix[2 * chip + 1 - c]).astype(BF16)


def own_side_prices(area, excess, matrix, partial):
    c = lax.rem(area[0], 2)
    for chip in range(partial.shape[0]):
        partial[chip] = nn(excess[...], matrix[2 * chip + c])


def both_sides(mine, other, *more):
    *extra, sent = more
    for chip in range(mine.shape[0]):
        total = (mine[chip] + other[chip].astype(F32)).astype(BF16)
        for copy in range(sent.shape[0]):
            sent[copy, chip] = total
    for ref in extra:
        for i in range(ref.shape[0]):
            for copy in range(sent.shape[0]):
                sent[copy, mine.shape[0] + i] = ref[i]


def own_side_flow(area, injection, matrix, base, flow):
    c = lax.rem(area[0], 2)
    for b in range(matrix.shape[1] // 256):
        lines = pl.ds(256 * b, 256)
        total = base[:, lines]
        for chip in range(injection.shape[0]):
            total = add_flow(total, injection[chip], matrix, 2 * chip + c, lines)
        flow[:, lines] = total


def other_side_flow(area, half_flow, mine, other, matrix, imb_base, cap, partial, imbalance, excess, flow):
    c = lax.rem(area[0], 2)
    chips = mine.shape[0]
    over = []
    for b in range(matrix.shape[1] // 256):
        lines = pl.ds(256 * b, 256)
        total = half_flow[:, lines]
        for chip in range(chips):
            total = add_flow(total, other[chip], matrix, 2 * chip + 1 - c, lines)
        flow[:, lines] = total
        over.append(excess_of(total, cap[:, lines]))
    over = jnp.concatenate(over, axis=1)
    excess[...] = over
    if partial.shape[0] == chips:
        for chip in range(chips):
            partial[chip] = nn(over, matrix[2 * chip + 1 - c]).astype(BF16)
    else:
        for a in range(2 * chips):
            partial[a] = nn(over, matrix[a]).astype(BF16)
    total = jnp.zeros(mine.shape[1:], F32)
    for chip in range(chips):
        total += mine[chip].astype(F32) + other[chip].astype(F32)
    imbalance[...] = imb_base[...] + lane_sum(total)


def moved(data, price, imbalance, commit, dispatch, w_comm, w_disp, comm_mean, disp_mean):
    linear, quadratic, fixed_cost, capacity = (data[i : i + 1] for i in range(4))
    grad = (
        linear
        + quadratic * dispatch
        + flow_weight * price
        + imbalance[:, :1] / BUSES
        + w_disp
        + penalty * (dispatch - disp_mean)
    )
    commit = jnp.clip(
        commit - commit_step * (fixed_cost - dispatch / capacity + w_comm + penalty * (commit - comm_mean)), 0.0, 1.0
    )
    step_gen = 1.0 / (quadratic + penalty + 2.0)
    return commit, jnp.clip(dispatch - step_gen * grad, 0.0, capacity * commit)


def summed(prices, at):
    total = prices[(0, *at)].astype(F32)
    for i in range(1, prices.shape[0]):
        total = total + prices[(i, *at)].astype(F32)
    return total


def first_update(prices, imbalance, data, same, outside_gen, first, commit_out, dispatch_out, injection):
    shape = dispatch_out.shape[1:]
    for chip in range(data.shape[0]):
        values = data[chip]
        start = jnp.broadcast_to(0.25 * values[3:4], shape)
        half = jnp.full(shape, 0.5, F32)
        commit, dispatch = moved(values, summed(prices, (chip,)), imbalance, half, start, 0.0, 0.0, half, start)
        commit_out[chip] = commit
        dispatch_out[chip] = dispatch
        injection[chip] = gen_injection(dispatch, same[chip], outside_gen[chip], first[chip])


def second_update(
    area, prices, imbalance, data, same, outside_gen, first, commit_in, dispatch_in, weight,
    commit_out, dispatch_out, injection, terms,
):
    rows = dispatch_in.shape[1]
    for chip in range(data.shape[0]):
        values = data[chip]
        start = jnp.broadcast_to(0.25 * values[3:4], dispatch_in.shape[1:])
        half = jnp.full(start.shape, 0.5, F32)
        commit, dispatch = moved(
            values, summed(prices, (chip,)), imbalance, commit_in[chip], dispatch_in[chip], 0.0, 0.0, half, start
        )
        injection[chip] = gen_injection(dispatch, same[chip], outside_gen[chip], first[chip])
        commit_out[chip] = commit
        dispatch_out[chip] = dispatch
    own = lax.div(area[0], 2)
    terms[:rows] = weight[:1] * commit_out[own]
    terms[rows : 2 * rows] = weight[:1] * dispatch_out[own]
    terms[2 * rows :] = weight[...]


def add_terms(*refs):
    refs[-1][...] = (refs[0][...] + refs[1][...]) + (refs[2][...] + refs[3][...])


def mean_kernel(weight, terms0, terms1, terms2, terms3, pieces, prob):
    total = (terms0[...] + terms1[...]) + (terms2[...] + terms3[...])
    rows = pieces.shape[1]
    prob[...] = weight[...] / total[2 * rows :]
    for i in range(2):
        mean = total[i * rows : (i + 1) * rows] / total[2 * rows : 2 * rows + 1]
        high = mean.astype(BF16)
        pieces[2 * i] = high
        pieces[2 * i + 1] = (mean - high.astype(F32)).astype(BF16)


def third_update(
    area, prices, imbalance, data, same, outside_gen, first, commit_in, dispatch_in, state, injection, kept,
):
    chips = data.shape[0]
    for chip in range(chips):
        comm_mean, disp_mean = (
            prices[chip, chips + i].astype(F32) + prices[chip, chips + i + 1].astype(F32) for i in (0, 2)
        )
        commit, dispatch = commit_in[chip], dispatch_in[chip]
        w_comm = penalty * (commit - comm_mean)
        w_disp = penalty * (dispatch - disp_mean)
        commit, dispatch = moved(
            data[chip], summed(prices, (chip,)), imbalance, commit, dispatch, w_comm, w_disp, comm_mean, disp_mean
        )
        injection[chip] = gen_injection(dispatch, same[chip], outside_gen[chip], first[chip])
        for i, value in enumerate((commit, dispatch, w_comm, w_disp, comm_mean, disp_mean)):
            kept[i, chip] = value
    own = lax.div(area[0], 2)
    for i in range(6):
        state[i] = kept[i, own]


def last_update(area, prices, imbalance, data, state, prob, dispatch_out, terms):
    commit, dispatch = moved(
        data[lax.div(area[0], 2)], summed(prices, ()), imbalance, *(state[i] for i in range(6))
    )
    dispatch_out[...] = dispatch
    share = prob[:1]
    commit = (share * (commit - state[4])).astype(BF16)
    dispatch = (share * (dispatch - state[5])).astype(BF16)
    for copy in range(terms.shape[0]):
        terms[copy, 0] = commit
        terms[copy, 1] = dispatch


def last_means(terms, state, comm_mean, disp_mean):
    comm_mean[...] = state[4] + summed(terms, (0,))
    disp_mean[...] = state[5] + summed(terms, (1,))


def call(kernel, outs, *args, mib=4, cost=1, scalars=0, **more):
    if scalars:
        memories = [pltpu.SMEM] * scalars + [pltpu.VMEM] * (len(args) - scalars)
        more["in_specs"] = [pl.BlockSpec(memory_space=memory) for memory in memories]
    return pl.pallas_call(
        kernel,
        out_shape=[jax.ShapeDtypeStruct(shape, dtype) for shape, dtype in outs],
        compiler_params=pltpu.CompilerParams(vmem_limit_bytes=mib * MIB),
        cost_estimate=pl.CostEstimate(flops=0, transcendentals=0, bytes_accessed=cost * 3_000_000),
        **more,
    )(*args)


def spread(copies, axis, groups=None):
    return lax.all_to_all(copies, axis, split_axis=0, concat_axis=0, tiled=True, axis_index_groups=groups)


def swapped(block, axis, bits):
    return lax.ppermute(block, axis, [(i, i ^ bits) for i in range(lax.axis_size(axis))])


def on_device(wind, load, ptdf_tiles, tile_cols, line_cap, gen_bus, gen_data, prob_weight):
    _, hours, buses = wind.shape
    gens = gen_bus.shape[0]
    lines = line_cap.shape[0]
    areas = lax.axis_size("area")
    scens = lax.axis_size("scen")
    chips = areas // 2
    area = lax.axis_index("area")[None]
    groups = [[2 * i + c for i in range(chips)] for c in range(2)]
    state = (hours, gens)

    [sent] = call(
        prepare_kernel,
        [((chips, 20, hours, 128), BF16)],
        area, wind[0], load, gen_bus[None, :], gen_data,
        mib=56, scalars=1,
    )
    sent = sent.reshape(chips, 4, 15, 8, 128).swapaxes(2, 3).reshape(chips, 32, 1920)
    mine = spread(sent, "area", groups)
    mine = mine.reshape(chips, 4, 8, 15, 128).swapaxes(2, 3).reshape(chips, 20, hours, 128)
    other = swapped(mine, "area", 1)
    *params, weight, cols, cap = call(
        params_kernel,
        [
            ((chips, 4, gens), F32),
            ((chips, gens, gens), BF16),
            ((chips, *state), F32),
            ((chips, 1, gens), F32),
            ((8, gens), F32),
            (tile_cols.shape, jnp.int32),
            ((1, lines), F32),
        ],
        prob_weight, mine, tile_cols, line_cap[None, :],
        mib=8, scalars=1,
    )

    def whole(shape):
        return pl.BlockSpec(shape, lambda k: (0,) * len(shape))

    starts = [
        ((areas, lines, gens), BF16),
        ((chips, *state), BF16),
        ((hours, lines), F32),
        ((hours, 128), F32),
        ((hours, 128), F32),
        ((hours, lines), BF16),
    ]
    matrix, partial, base, imb_base, imbalance, excess = call(
        start_kernel,
        starts,
        cols, area, ptdf_tiles, mine, other, cap,
        mib=40, cost=16,
        grid=(ptdf_tiles.shape[0],),
        in_specs=[
            pl.BlockSpec(memory_space=pltpu.SMEM),
            pl.BlockSpec(memory_space=pltpu.SMEM),
            pl.BlockSpec((1, *ptdf_tiles.shape[1:]), lambda k: (k, 0, 0, 0)),
            whole(mine.shape),
            whole(other.shape),
            whole(cap.shape),
        ],
        out_specs=[whole(shape) for shape, _ in starts],
        scratch_shapes=[pltpu.VMEM((areas, 16, hours, 128), BF16), pltpu.VMEM((areas, 1, gens), F32)],
    )

    def all_prices(partial, excess, *more):
        theirs = swapped(partial, "area", 1)
        [ours] = call(own_side_prices, [((chips, *state), F32)], area, excess, matrix, cost=2, scalars=1)
        count = chips + sum(a.shape[0] for a in more)
        [sent] = call(both_sides, [((chips, count, *state), BF16)], ours, theirs, *more)
        tiles = sent.reshape(chips, 3 * count, 8, 2, 128).swapaxes(2, 3)
        row = max(n for n in range(1, 17) if 6 * count % n == 0)
        sent = tiles.reshape(chips, -1, row, 8, 128).swapaxes(2, 3).reshape(chips, -1, 128 * row)
        got = spread(sent, "area", groups)
        got = got.reshape(chips, -1, 8, row, 128).swapaxes(2, 3).reshape(chips, 3 * count, 2, 8, 128)
        return got.swapaxes(2, 3).reshape(chips, count, *state)

    def flow_and_prices(injection, count, *near):
        theirs = swapped(injection, "area", 1)
        [half] = call(own_side_flow, [((hours, lines), F32)], area, injection, matrix, base, cost=2, scalars=1)
        far = ()
        if near:
            half, theirs, *near = lax.optimization_barrier((half, theirs, *near))
            [terms] = call(add_terms, [(near[0].shape, F32)], *near)
            far = [terms] + [swapped(terms, "scen", bits) for bits in (2, 4, 6)]
        out = call(
            other_side_flow,
            [((count, *state), BF16), ((hours, 128), F32), ((hours, lines), BF16), ((hours, lines), F32)],
            area, half, injection, theirs, matrix, imb_base, cap,
            cost=3, scalars=1,
        )
        return (*out, *far)

    eight = ((chips, *state), F32)
    eights = [eight, eight, ((chips, *state), BF16)]
    commit, dispatch, injection = call(
        first_update,
        eights,
        all_prices(partial, excess), imbalance, *params,
        mib=8,
    )
    partial, imbalance, excess, _ = flow_and_prices(injection, chips)
    terms_of = ((2 * hours + 8, gens), F32)
    commit, dispatch, injection, terms = call(
        second_update,
        [*eights, terms_of],
        area, all_prices(partial, excess), imbalance, *params, commit, dispatch, weight,
        mib=8, scalars=1,
    )
    near = [terms] + [swapped(terms, "scen", bits) for bits in (scens // 2, 1, scens // 2 + 1)]
    partial, imbalance, excess, _, *far = flow_and_prices(injection, chips, *near)
    pieces, prob = call(
        mean_kernel,
        [((4, *state), BF16), ((8, gens), F32)],
        weight, *far,
    )
    kept, injection = call(
        third_update,
        [((6, *state), F32), ((chips, *state), BF16)],
        area, all_prices(partial, excess, pieces), imbalance, *params, commit, dispatch,
        mib=8, scalars=1,
        scratch_shapes=[pltpu.VMEM((6, chips, *state), F32)],
    )
    partial, imbalance, _, flow = flow_and_prices(injection, areas)
    dispatch, terms = call(
        last_update,
        [(state, F32), ((scens, 2, *state), BF16)],
        area, spread(partial, "area"), imbalance, params[0], kept, prob,
        scalars=1,
    )
    comm_mean, disp_mean = call(last_means, [(state, F32), (state, F32)], spread(terms, "scen"), kept)
    return comm_mean, disp_mean, dispatch[None], flow[None]


def solution(mesh):
    placed = (
        P("scen", None, "area"),
        P(None, "area"),
        P("area", None, None, None),
        P("area", None),
        P("area"),
        P("area"),
        P(None, "area"),
        P("scen"),
    )
    return jax.shard_map(
        on_device,
        mesh=mesh,
        in_specs=placed,
        out_specs=(
            P(None, "area"),
            P(None, "area"),
            P("scen", None, "area"),
            P("scen", None, "area"),
        ),
        check_vma=False,
    )
```

```python
import jax
import jax.numpy as jnp
from jax import lax
from jax.experimental import pallas as pl
from jax.experimental.pallas import tpu as pltpu
from jax.sharding import PartitionSpec as P

BUSES = 24576
penalty = 1.0
flow_weight = 0.25
commit_step = 0.5
F32 = jnp.float32
BF16 = jnp.bfloat16
MIB = 1 << 20


def nt(a, b):
    return lax.dot_general(a, b, (((1,), (1,)), ((), ())), preferred_element_type=F32)


def nn(a, b):
    return jnp.dot(a, b, preferred_element_type=F32)


def at_shared_buses(dispatch, same):
    high = dispatch.astype(BF16)
    rest = dispatch - high.astype(F32)
    middle = rest.astype(BF16)
    low = (rest - middle.astype(F32)).astype(BF16)
    return nn(high, same) + (nn(middle, same) + nn(low, same))


def gen_injection(dispatch, same, outside_gen, first):
    placed = at_shared_buses(dispatch, same)
    return jnp.where(first > 0.5, placed + outside_gen, 0.0).astype(BF16)


def first_of(shared):
    gens = shared.shape[0]
    earlier = shared & (
        lax.broadcasted_iota(jnp.int32, (gens, gens), 0) < lax.broadcasted_iota(jnp.int32, (gens, gens), 1)
    )
    return 1.0 - jnp.max(earlier.astype(F32), axis=0, keepdims=True)


def as_column(row):
    return jnp.transpose(jnp.broadcast_to(row, (128, row.shape[1])))[:, :1]


def pieces_of(values):
    high = values.astype(BF16).astype(F32)
    middle = (values - high).astype(BF16).astype(F32)
    return high, middle, values - high - middle


def stacked(lines, rows):
    line = lax.broadcasted_iota(jnp.int32, (rows, lines[0].shape[1]), 0)
    out = jnp.zeros(line.shape, F32)
    for i, values in enumerate(lines):
        out = jnp.where(line == i, values, out)
    return out.astype(BF16)


def prepare_kernel(area, wind, load, bus, data, sent):
    rows, buses = wind.shape
    gens = bus.shape[1]
    row_int = bus[...] - area[0] * buses
    row = row_int.astype(F32)
    col = as_column(row)
    onehot = (col == lax.broadcasted_iota(jnp.int32, (gens, buses), 1).astype(F32)).astype(F32).astype(BF16)
    held = nn(jnp.ones((8, gens), BF16), onehot)[:1]
    wind_gen, load_gen = nt(wind[...], onehot), nt(load[...], onehot)
    shared = col == row
    dispatch = jnp.broadcast_to(0.25 * data[3:4, :], (rows, gens))
    injection = gen_injection(dispatch, shared.astype(F32).astype(BF16), wind_gen - load_gen, first_of(shared))
    base = jnp.where(held > 0.5, 0.0, wind[...].astype(F32) - load[...].astype(F32)).astype(BF16)
    tile_at = row_int // 128
    lane_at = (row_int - 128 * tile_at).astype(F32)
    lines = [tile_at.astype(F32), lane_at]
    for i in range(4):
        lines.extend(pieces_of(data[i : i + 1, :]))
    wind_gen, load_gen = wind_gen.astype(BF16), load_gen.astype(BF16)
    for half in range(2):
        lanes = slice(128 * half, 128 * (half + 1))
        info = stacked([values[:, lanes] for values in lines], rows)
        for copy in range(sent.shape[0]):
            sent[copy, 12 + half] = injection[:, lanes]
            sent[copy, 14 + half] = info
            sent[copy, 16 + half] = wind_gen[:, lanes]
            sent[copy, 18 + half] = load_gen[:, lanes]
    for copy in range(sent.shape[0]):
        for j in range(12):
            sent[copy, j] = base[:, 128 * j : 128 * (j + 1)]


def side_by_side(blocks, *at):
    left, right = blocks[at].astype(F32), blocks[(*at[:-1], at[-1] + 1)].astype(F32)
    return jnp.concatenate([left, right], axis=1)


def params_kernel(prob_weight, mine, cols, cap, data, same, outside_gen, first, weight, cols_out, cap_out):
    cols_out[...] = cols[...]
    cap_out[...] = cap[...]
    weight[...] = jnp.full(weight.shape, prob_weight[0].astype(F32))
    for chip in range(mine.shape[0]):
        info = side_by_side(mine, chip, 14)
        bus = info[0:1] * 128.0 + info[1:2]
        shared = as_column(bus) == bus
        same[chip] = shared.astype(F32).astype(BF16)
        first[chip] = first_of(shared)
        for i in range(4):
            at = 2 + 3 * i
            data[chip, i : i + 1] = info[at : at + 1] + info[at + 1 : at + 2] + info[at + 2 : at + 3]
        outside_gen[chip] = side_by_side(mine, chip, 16) - side_by_side(mine, chip, 18)


def add_flow(total, inject, matrix, area, rows):
    return total + nt(inject, matrix[area, rows, :])


def excess_of(flow, limit):
    return (flow - jnp.clip(flow, -limit, limit)).astype(BF16)


def lane_sum(total):
    return jnp.broadcast_to(jnp.sum(total, axis=1, keepdims=True), (total.shape[0], 128))


def start_kernel(
    cols, area, tiles, mine, other, cap,
    matrix, partial, base, imb_base, imbalance, excess, held, code,
):
    k = pl.program_id(0)
    areas = matrix.shape[0]
    rows = held.shape[2]
    c = lax.rem(area[0], 2)

    @pl.when(k == 0)
    def _():
        for chip in range(areas // 2):
            for j in range(16):
                held[2 * chip + c, j] = mine[chip, j]
                held[2 * chip + 1 - c, j] = other[chip, j]
        total = jnp.zeros((rows, 128), F32)
        gen_total = jnp.zeros((rows, 128), F32)
        for a in range(areas):
            for j in range(12):
                total += held[a, j].astype(F32)
            for j in range(12, 14):
                gen_total += held[a, j].astype(F32)
            info = side_by_side(held, a, 14)
            code[a] = info[0:1] * 128.0 + info[1:2]
        before = lane_sum(total)
        imb_base[...] = before
        imbalance[...] = before + lane_sum(gen_total)
        matrix[...] = jnp.zeros_like(matrix)

    at_bus = lax.broadcasted_iota(jnp.int32, (128, 256), 0).astype(F32)
    here = pl.ds(pl.multiple_of(k * 128, 128), 128)

    total = jnp.zeros((rows, 128), F32)
    for z in range(tiles.shape[1]):
        t = cols[k, z]
        a = t // 12
        j = t - 12 * a
        tile = tiles[0, z]
        total = total + nt(held[a, j], tile)
        bus = code[a] - (128 * j).astype(F32)
        pick = jnp.where(at_bus == bus, 1.0, 0.0).astype(BF16)
        matrix[a, here, :] = matrix[a, here, :] + nn(tile, pick).astype(BF16)
    base[:, here] = total

    @pl.when(k == pl.num_programs(0) - 1)
    def _():
        over = []
        for b in range(matrix.shape[1] // 256):
            lines = pl.ds(256 * b, 256)
            flow = base[:, lines]
            for a in range(areas):
                inject = jnp.concatenate([held[a, 12], held[a, 13]], axis=1)
                flow = add_flow(flow, inject, matrix, a, lines)
            over.append(excess_of(flow, cap[:, lines]))
        over = jnp.concatenate(over, axis=1)
        excess[...] = over
        for chip in range(areas // 2):
            partial[chip] = nn(over, matrix[2 * chip + 1 - c]).astype(BF16)


def own_side_prices(area, excess, matrix, partial):
    c = lax.rem(area[0], 2)
    for chip in range(partial.shape[0]):
        partial[chip] = nn(excess[...], matrix[2 * chip + c])


def both_sides(mine, other, total):
    for chip in range(mine.shape[0]):
        total[chip] = (mine[chip] + other[chip].astype(F32)).astype(BF16)


def sum_of_four(a, b, c, d, total):
    total[...] = ((a[...].astype(F32) + b[...].astype(F32)) + (c[...].astype(F32) + d[...].astype(F32))).astype(BF16)


def by_column(area, mine, other, kept, *sent):
    x = lax.rem(lax.div(area[0], 2), 4)
    for bits, ref in enumerate((kept, *sent)):
        for y in range(2):
            chip = 4 * y + lax.bitwise_xor(x, bits)
            ref[y] = (mine[chip] + other[chip].astype(F32)).astype(BF16)


def by_row(area, a, b, c, d, kept, sent):
    y = lax.div(area[0], 8)
    for at, ref in ((y, kept), (1 - y, sent)):
        total = (a[at].astype(F32) + b[at].astype(F32)) + (c[at].astype(F32) + d[at].astype(F32))
        ref[...] = total.astype(ref.dtype)


def own_side_flow(area, injection, matrix, base, flow):
    c = lax.rem(area[0], 2)
    for b in range(matrix.shape[1] // 256):
        lines = pl.ds(256 * b, 256)
        total = base[:, lines]
        for chip in range(injection.shape[0]):
            total = add_flow(total, injection[chip], matrix, 2 * chip + c, lines)
        flow[:, lines] = total


def other_side_flow(area, half_flow, mine, other, matrix, imb_base, cap, partial, imbalance, excess):
    c = lax.rem(area[0], 2)
    chips = mine.shape[0]
    over = []
    for b in range(matrix.shape[1] // 256):
        lines = pl.ds(256 * b, 256)
        total = half_flow[:, lines]
        for chip in range(chips):
            total = add_flow(total, other[chip], matrix, 2 * chip + 1 - c, lines)
        over.append(excess_of(total, cap[:, lines]))
    over = jnp.concatenate(over, axis=1)
    excess[...] = over
    for chip in range(chips):
        partial[chip] = nn(over, matrix[2 * chip + 1 - c]).astype(BF16)
    total = jnp.zeros(mine.shape[1:], F32)
    for chip in range(chips):
        total += mine[chip].astype(F32) + other[chip].astype(F32)
    imbalance[...] = imb_base[...] + lane_sum(total)


def step_kernel(injection, matrix, base, imb_base, cap, partial, imbalance, flow):
    areas, lines, _ = matrix.shape
    over = []
    for b in range(lines // 256):
        rows = pl.ds(256 * b, 256)
        total = base[:, rows]
        for a in range(areas):
            total = add_flow(total, injection[a], matrix, a, rows)
        flow[:, rows] = total
        over.append(excess_of(total, cap[:, rows]))
    over = jnp.concatenate(over, axis=1)
    for a in range(areas):
        partial[a] = nn(over, matrix[a]).astype(BF16)
    total = jnp.zeros(injection.shape[1:], F32)
    for a in range(areas):
        total += injection[a].astype(F32)
    imbalance[...] = imb_base[...] + lane_sum(total)


def moved(data, price, imbalance, commit, dispatch, w_comm, w_disp, comm_mean, disp_mean):
    linear, quadratic, fixed_cost, capacity = (data[i : i + 1] for i in range(4))
    grad = (
        linear
        + quadratic * dispatch
        + flow_weight * price
        + imbalance[:, :1] / BUSES
        + w_disp
        + penalty * (dispatch - disp_mean)
    )
    commit = jnp.clip(
        commit - commit_step * (fixed_cost - dispatch / capacity + w_comm + penalty * (commit - comm_mean)), 0.0, 1.0
    )
    step_gen = 1.0 / (quadratic + penalty + 2.0)
    return commit, jnp.clip(dispatch - step_gen * grad, 0.0, capacity * commit)


def summed(prices, at):
    total = prices[(0, *at)].astype(F32)
    for i in range(1, prices.shape[0]):
        total = total + prices[(i, *at)].astype(F32)
    return total


def first_update(near, far, imbalance, data, same, outside_gen, first, commit_out, dispatch_out, injection):
    shape = dispatch_out.shape[1:]
    for chip in range(data.shape[0]):
        values = data[chip]
        start = jnp.broadcast_to(0.25 * values[3:4], shape)
        half = jnp.full(shape, 0.5, F32)
        commit, dispatch = moved(values, near[chip].astype(F32) + far[chip].astype(F32), imbalance, half, start, 0.0, 0.0, half, start)
        commit_out[chip] = commit
        dispatch_out[chip] = dispatch
        injection[chip] = gen_injection(dispatch, same[chip], outside_gen[chip], first[chip])


def second_update(
    area, near, far, imbalance, data, same, outside_gen, first, commit_in, dispatch_in, weight,
    state_out, injection, terms, kept,
):
    shape = dispatch_in.shape[1:]
    for chip in range(data.shape[0]):
        values = data[chip]
        start = jnp.broadcast_to(0.25 * values[3:4], shape)
        half = jnp.full(shape, 0.5, F32)
        commit, dispatch = moved(
            values, near[chip].astype(F32) + far[chip].astype(F32), imbalance, commit_in[chip], dispatch_in[chip], 0.0, 0.0, half, start
        )
        injection[chip] = gen_injection(dispatch, same[chip], outside_gen[chip], first[chip])
        kept[0, chip] = commit
        kept[1, chip] = dispatch
    rows = shape[0]
    for i in range(2):
        value = kept[i, lax.div(area[0], 2)]
        state_out[i] = value
        terms[i * rows : (i + 1) * rows] = weight[:1] * value
    terms[2 * rows :] = weight[...]


def add_terms(*refs):
    refs[-1][...] = (refs[0][...] + refs[1][...]) + (refs[2][...] + refs[3][...])


def third_update(
    area, near, far, imbalance, data, same, outside_gen, first, state, weight, terms0, terms1, terms2, terms3,
    state_out, sent, means, prob,
):
    commit, dispatch = state[0], state[1]
    total = (terms0[...] + terms1[...]) + (terms2[...] + terms3[...])
    rows = commit.shape[0]
    weights = total[2 * rows : 2 * rows + 1]
    comm_mean, disp_mean = total[:rows] / weights, total[rows : 2 * rows] / weights
    prob[...] = weight[...] / total[2 * rows :]
    w_comm = penalty * (commit - comm_mean)
    w_disp = penalty * (dispatch - disp_mean)
    means[0] = comm_mean
    means[1] = disp_mean
    me = lax.div(area[0], 2)
    commit, dispatch = moved(
        data[me], near[...] + far[...].astype(F32), imbalance, commit, dispatch, w_comm, w_disp, comm_mean, disp_mean
    )
    state_out[0] = commit
    state_out[1] = dispatch
    state_out[2] = w_comm
    state_out[3] = w_disp
    injection = gen_injection(dispatch, same[me], outside_gen[me], first[me])
    for copy in range(sent.shape[0]):
        sent[copy] = injection


def last_update(area, prices, imbalance, data, state, means, prob, dispatch_out, terms):
    commit, dispatch = moved(
        data[lax.div(area[0], 2)], summed(prices, ()), imbalance, state[0], state[1], state[2], state[3], means[0], means[1]
    )
    dispatch_out[...] = dispatch
    share = prob[:1]
    commit = (share * (commit - means[0])).astype(BF16)
    dispatch = (share * (dispatch - means[1])).astype(BF16)
    for copy in range(terms.shape[0]):
        terms[copy, 0] = commit
        terms[copy, 1] = dispatch


def last_means(terms, means, comm_mean, disp_mean):
    comm_mean[...] = means[0] + summed(terms, (0,))
    disp_mean[...] = means[1] + summed(terms, (1,))


def call(kernel, outs, *args, mib=4, cost=1, scalars=0, **more):
    if scalars:
        memories = [pltpu.SMEM] * scalars + [pltpu.VMEM] * (len(args) - scalars)
        more["in_specs"] = [pl.BlockSpec(memory_space=memory) for memory in memories]
    return pl.pallas_call(
        kernel,
        out_shape=[jax.ShapeDtypeStruct(shape, dtype) for shape, dtype in outs],
        compiler_params=pltpu.CompilerParams(vmem_limit_bytes=mib * MIB),
        cost_estimate=pl.CostEstimate(flops=0, transcendentals=0, bytes_accessed=cost * 3_000_000),
        **more,
    )(*args)


def spread(copies, axis, groups=None):
    return lax.all_to_all(copies, axis, split_axis=0, concat_axis=0, tiled=True, axis_index_groups=groups)


def swapped(block, axis, bits):
    return lax.ppermute(block, axis, [(i, i ^ bits) for i in range(lax.axis_size(axis))])


def on_device(wind, load, ptdf_tiles, tile_cols, line_cap, gen_bus, gen_data, prob_weight):
    _, hours, buses = wind.shape
    gens = gen_bus.shape[0]
    lines = line_cap.shape[0]
    areas = lax.axis_size("area")
    scens = lax.axis_size("scen")
    chips = areas // 2
    area = lax.axis_index("area")[None]
    groups = [[2 * i + c for i in range(chips)] for c in range(2)]
    state = (hours, gens)

    [sent] = call(
        prepare_kernel,
        [((chips, 20, hours, 128), BF16)],
        area, wind[0], load, gen_bus[None, :], gen_data,
        mib=56, scalars=1,
    )
    mine = spread(sent, "area", groups)
    other = swapped(mine, "area", 1)
    *params, weight, cols, cap = call(
        params_kernel,
        [
            ((chips, 4, gens), F32),
            ((chips, gens, gens), BF16),
            ((chips, *state), F32),
            ((chips, 1, gens), F32),
            ((8, gens), F32),
            (tile_cols.shape, jnp.int32),
            ((1, lines), F32),
        ],
        prob_weight, mine, tile_cols, line_cap[None, :],
        mib=8, scalars=1,
    )

    def whole(shape):
        return pl.BlockSpec(shape, lambda k: (0,) * len(shape))

    starts = [
        ((areas, lines, gens), BF16),
        ((chips, *state), BF16),
        ((hours, lines), F32),
        ((hours, 128), F32),
        ((hours, 128), F32),
        ((hours, lines), BF16),
    ]
    matrix, partial, base, imb_base, imbalance, excess = call(
        start_kernel,
        starts,
        cols, area, ptdf_tiles, mine, other, cap,
        mib=40, cost=16,
        grid=(ptdf_tiles.shape[0],),
        in_specs=[
            pl.BlockSpec(memory_space=pltpu.SMEM),
            pl.BlockSpec(memory_space=pltpu.SMEM),
            pl.BlockSpec((1, *ptdf_tiles.shape[1:]), lambda k: (k, 0, 0, 0)),
            whole(mine.shape),
            whole(other.shape),
            whole(cap.shape),
        ],
        out_specs=[whole(shape) for shape, _ in starts],
        scratch_shapes=[pltpu.VMEM((areas, 16, hours, 128), BF16), pltpu.VMEM((areas, 1, gens), F32)],
    )

    def both_cores(partial, excess):
        theirs = swapped(partial, "area", 1)
        [ours] = call(own_side_prices, [((chips, *state), F32)], area, excess, matrix, cost=2, scalars=1)
        return ours, theirs

    def all_prices(partial, excess):
        [total] = call(both_sides, [((chips, *state), BF16)], *both_cores(partial, excess))
        along_x = [swapped(total, "area", bits) for bits in (2, 4, 6)]
        [total] = call(sum_of_four, [((chips, *state), BF16)], total, *along_x)
        return total, swapped(total, "area", 8)

    def own_prices(partial, excess):
        kept, *sent = call(
            by_column, [((2, *state), BF16)] * 4, area, *both_cores(partial, excess), scalars=1
        )
        along_x = [swapped(block, "area", bits) for block, bits in zip(sent, (2, 4, 6))]
        kept, sent = call(by_row, [(state, F32), (state, BF16)], area, kept, *along_x, scalars=1)
        return kept, swapped(sent, "area", 8)

    def flow_and_prices(injection):
        theirs = swapped(injection, "area", 1)
        [half] = call(own_side_flow, [((hours, lines), F32)], area, injection, matrix, base, cost=2, scalars=1)
        return call(
            other_side_flow,
            [((chips, *state), BF16), ((hours, 128), F32), ((hours, lines), BF16)],
            area, half, injection, theirs, matrix, imb_base, cap,
            cost=3, scalars=1,
        )

    eight = ((chips, *state), F32)
    commit, dispatch, injection = call(
        first_update,
        [eight, eight, ((chips, *state), BF16)],
        *all_prices(partial, excess), imbalance, *params,
        mib=8,
    )
    partial, imbalance, excess = flow_and_prices(injection)
    kept, injection, terms = call(
        second_update,
        [((2, *state), F32), ((chips, *state), BF16), ((2 * hours + 8, gens), F32)],
        area, *all_prices(partial, excess), imbalance, *params, commit, dispatch, weight,
        mib=8, scalars=1,
        scratch_shapes=[pltpu.VMEM((2, chips, *state), F32)],
    )
    near = [terms] + [swapped(terms, "scen", bits) for bits in (scens // 2, 1, scens // 2 + 1)]
    partial, imbalance, excess = flow_and_prices(injection)
    [terms] = call(add_terms, [(terms.shape, F32)], *near)
    partial, excess, terms = lax.optimization_barrier((partial, excess, terms))
    far = [terms] + [swapped(terms, "scen", bits) for bits in (2, 4, 6)]
    kept, sent, means, prob = call(
        third_update,
        [((4, *state), F32), ((areas, *state), BF16), ((2, *state), F32), ((8, gens), F32)],
        area, *own_prices(partial, excess), imbalance, *params, kept, weight, *far,
        scalars=1,
    )
    partial, imbalance, flow = call(
        step_kernel,
        [((areas, *state), BF16), ((hours, 128), F32), ((hours, lines), F32)],
        spread(sent, "area"), matrix, base, imb_base, cap,
        mib=6, cost=5,
    )
    dispatch, terms = call(
        last_update,
        [(state, F32), ((scens, 2, *state), BF16)],
        area, spread(partial, "area"), imbalance, params[0], kept, means, prob,
        scalars=1,
    )
    comm_mean, disp_mean = call(last_means, [(state, F32), (state, F32)], spread(terms, "scen"), means)
    return comm_mean, disp_mean, dispatch[None], flow[None]


def solution(mesh):
    placed = (
        P("scen", None, "area"),
        P(None, "area"),
        P("area", None, None, None),
        P("area", None),
        P("area"),
        P("area"),
        P(None, "area"),
        P("scen"),
    )
    return jax.shard_map(
        on_device,
        mesh=mesh,
        in_specs=placed,
        out_specs=(
            P(None, "area"),
            P(None, "area"),
            P("scen", None, "area"),
            P("scen", None, "area"),
        ),
        check_vma=False,
    )
```

```python
import jax
import jax.numpy as jnp
from jax import lax
from jax.experimental import pallas as pl
from jax.experimental.pallas import tpu as pltpu
from jax.sharding import PartitionSpec as P

BUSES = 24576
penalty = 1.0
flow_weight = 0.25
commit_step = 0.5
F32 = jnp.float32
BF16 = jnp.bfloat16
MIB = 1 << 20


def nt(a, b):
    return lax.dot_general(a, b, (((1,), (1,)), ((), ())), preferred_element_type=F32)


def nn(a, b):
    return jnp.dot(a, b, preferred_element_type=F32)


def at_shared_buses(dispatch, same):
    high = dispatch.astype(BF16)
    rest = dispatch - high.astype(F32)
    middle = rest.astype(BF16)
    low = (rest - middle.astype(F32)).astype(BF16)
    return nn(high, same) + (nn(middle, same) + nn(low, same))


def gen_injection(dispatch, same, outside_gen, first):
    placed = at_shared_buses(dispatch, same)
    return jnp.where(first > 0.5, placed + outside_gen, 0.0).astype(BF16)


def first_of(shared):
    gens = shared.shape[0]
    earlier = shared & (
        lax.broadcasted_iota(jnp.int32, (gens, gens), 0) < lax.broadcasted_iota(jnp.int32, (gens, gens), 1)
    )
    return 1.0 - jnp.max(earlier.astype(F32), axis=0, keepdims=True)


def as_column(row):
    return jnp.transpose(jnp.broadcast_to(row, (128, row.shape[1])))[:, :1]


def pieces_of(values):
    high = values.astype(BF16).astype(F32)
    middle = (values - high).astype(BF16).astype(F32)
    return high, middle, values - high - middle


def stacked(lines, rows):
    line = lax.broadcasted_iota(jnp.int32, (rows, lines[0].shape[1]), 0)
    out = jnp.zeros(line.shape, F32)
    for i, values in enumerate(lines):
        out = jnp.where(line == i, values, out)
    return out.astype(BF16)


def prepare_kernel(area, wind, load, bus, data, sent):
    rows, buses = wind.shape
    gens = bus.shape[1]
    row_int = bus[...] - area[0] * buses
    row = row_int.astype(F32)
    col = as_column(row)
    onehot = (col == lax.broadcasted_iota(jnp.int32, (gens, buses), 1).astype(F32)).astype(F32).astype(BF16)
    held = nn(jnp.ones((8, gens), BF16), onehot)[:1]
    wind_gen, load_gen = nt(wind[...], onehot), nt(load[...], onehot)
    shared = col == row
    dispatch = jnp.broadcast_to(0.25 * data[3:4, :], (rows, gens))
    injection = gen_injection(dispatch, shared.astype(F32).astype(BF16), wind_gen - load_gen, first_of(shared))
    base = jnp.where(held > 0.5, 0.0, wind[...].astype(F32) - load[...].astype(F32)).astype(BF16)
    tile_at = row_int // 128
    lane_at = (row_int - 128 * tile_at).astype(F32)
    lines = [tile_at.astype(F32), lane_at]
    for i in range(4):
        lines.extend(pieces_of(data[i : i + 1, :]))
    wind_gen, load_gen = wind_gen.astype(BF16), load_gen.astype(BF16)
    for half in range(2):
        lanes = slice(128 * half, 128 * (half + 1))
        info = stacked([values[:, lanes] for values in lines], rows)
        for copy in range(sent.shape[0]):
            sent[copy, 12 + half] = injection[:, lanes]
            sent[copy, 14 + half] = info
            sent[copy, 16 + half] = wind_gen[:, lanes]
            sent[copy, 18 + half] = load_gen[:, lanes]
    for copy in range(sent.shape[0]):
        for j in range(12):
            sent[copy, j] = base[:, 128 * j : 128 * (j + 1)]


def side_by_side(blocks, *at):
    left, right = blocks[at].astype(F32), blocks[(*at[:-1], at[-1] + 1)].astype(F32)
    return jnp.concatenate([left, right], axis=1)


def params_kernel(prob_weight, mine, cols, cap, data, same, outside_gen, first, weight, cols_out, cap_out):
    cols_out[...] = cols[...]
    cap_out[...] = cap[...]
    weight[...] = jnp.full(weight.shape, prob_weight[0].astype(F32))
    for chip in range(mine.shape[0]):
        info = side_by_side(mine, chip, 14)
        bus = info[0:1] * 128.0 + info[1:2]
        shared = as_column(bus) == bus
        same[chip] = shared.astype(F32).astype(BF16)
        first[chip] = first_of(shared)
        for i in range(4):
            at = 2 + 3 * i
            data[chip, i : i + 1] = info[at : at + 1] + info[at + 1 : at + 2] + info[at + 2 : at + 3]
        outside_gen[chip] = side_by_side(mine, chip, 16) - side_by_side(mine, chip, 18)


def add_flow(total, inject, matrix, area, rows):
    return total + nt(inject, matrix[area, rows, :])


def excess_of(flow, limit):
    return (flow - jnp.clip(flow, -limit, limit)).astype(BF16)


def lane_sum(total):
    return jnp.broadcast_to(jnp.sum(total, axis=1, keepdims=True), (total.shape[0], 128))


def start_kernel(
    cols, area, tiles, mine, other, cap,
    matrix, partial, base, imb_base, imbalance, excess, held, code,
):
    k = pl.program_id(0)
    areas = matrix.shape[0]
    rows = held.shape[2]
    c = lax.rem(area[0], 2)

    @pl.when(k == 0)
    def _():
        for chip in range(areas // 2):
            for j in range(16):
                held[2 * chip + c, j] = mine[chip, j]
                held[2 * chip + 1 - c, j] = other[chip, j]
        total = jnp.zeros((rows, 128), F32)
        gen_total = jnp.zeros((rows, 128), F32)
        for a in range(areas):
            for j in range(12):
                total += held[a, j].astype(F32)
            for j in range(12, 14):
                gen_total += held[a, j].astype(F32)
            info = side_by_side(held, a, 14)
            code[a] = info[0:1] * 128.0 + info[1:2]
        before = lane_sum(total)
        imb_base[...] = before
        imbalance[...] = before + lane_sum(gen_total)
        matrix[...] = jnp.zeros_like(matrix)

    at_bus = lax.broadcasted_iota(jnp.int32, (128, 256), 0).astype(F32)
    here = pl.ds(pl.multiple_of(k * 128, 128), 128)

    total = jnp.zeros((rows, 128), F32)
    for z in range(tiles.shape[1]):
        t = cols[k, z]
        a = t // 12
        j = t - 12 * a
        tile = tiles[0, z]
        total = total + nt(held[a, j], tile)
        bus = code[a] - (128 * j).astype(F32)
        pick = jnp.where(at_bus == bus, 1.0, 0.0).astype(BF16)
        matrix[a, here, :] = matrix[a, here, :] + nn(tile, pick).astype(BF16)
    base[:, here] = total

    @pl.when(k == pl.num_programs(0) - 1)
    def _():
        over = []
        for b in range(matrix.shape[1] // 256):
            lines = pl.ds(256 * b, 256)
            flow = base[:, lines]
            for a in range(areas):
                inject = jnp.concatenate([held[a, 12], held[a, 13]], axis=1)
                flow = add_flow(flow, inject, matrix, a, lines)
            over.append(excess_of(flow, cap[:, lines]))
        over = jnp.concatenate(over, axis=1)
        excess[...] = over
        for chip in range(areas // 2):
            partial[chip] = nn(over, matrix[2 * chip + 1 - c]).astype(BF16)


def own_side_prices(area, excess, matrix, partial):
    c = lax.rem(area[0], 2)
    for chip in range(partial.shape[0]):
        partial[chip] = nn(excess[...], matrix[2 * chip + c])


def both_sides(mine, other, *more):
    *extra, total = more
    chips = mine.shape[0]
    for chip in range(chips):
        total[chip] = (mine[chip] + other[chip].astype(F32)).astype(BF16)
    for ref in extra:
        for i in range(ref.shape[0]):
            total[chips + i] = ref[i]


def sum_of_four(area, *refs):
    *refs, total = refs
    a, b, c, d = refs
    chips = total.shape[0] if total.shape == a.shape else 2 * len(refs)
    for i in range(chips):
        pairs = (a[i].astype(F32) + b[i].astype(F32)) + (c[i].astype(F32) + d[i].astype(F32))
        total[i] = pairs.astype(BF16)
    count = a.shape[0] - chips
    for bits, ref in enumerate(refs):
        x = lax.bitwise_xor(lax.rem(lax.div(area[0], 2), 4), bits)
        for i in range(count):
            total[chips + count * x + i] = ref[chips + i]


def own_side_flow(area, injection, matrix, base, flow):
    c = lax.rem(area[0], 2)
    for b in range(matrix.shape[1] // 256):
        lines = pl.ds(256 * b, 256)
        total = base[:, lines]
        for chip in range(injection.shape[0]):
            total = add_flow(total, injection[chip], matrix, 2 * chip + c, lines)
        flow[:, lines] = total


def other_side_flow(area, half_flow, mine, other, matrix, imb_base, cap, partial, imbalance, excess, flow):
    c = lax.rem(area[0], 2)
    chips = mine.shape[0]
    over = []
    for b in range(matrix.shape[1] // 256):
        lines = pl.ds(256 * b, 256)
        total = half_flow[:, lines]
        for chip in range(chips):
            total = add_flow(total, other[chip], matrix, 2 * chip + 1 - c, lines)
        flow[:, lines] = total
        over.append(excess_of(total, cap[:, lines]))
    over = jnp.concatenate(over, axis=1)
    excess[...] = over
    if partial.shape[0] == chips:
        for chip in range(chips):
            partial[chip] = nn(over, matrix[2 * chip + 1 - c]).astype(BF16)
    else:
        for a in range(2 * chips):
            partial[a] = nn(over, matrix[a]).astype(BF16)
    total = jnp.zeros(mine.shape[1:], F32)
    for chip in range(chips):
        total += mine[chip].astype(F32) + other[chip].astype(F32)
    imbalance[...] = imb_base[...] + lane_sum(total)


def moved(data, price, imbalance, commit, dispatch, w_comm, w_disp, comm_mean, disp_mean):
    linear, quadratic, fixed_cost, capacity = (data[i : i + 1] for i in range(4))
    grad = (
        linear
        + quadratic * dispatch
        + flow_weight * price
        + imbalance[:, :1] / BUSES
        + w_disp
        + penalty * (dispatch - disp_mean)
    )
    commit = jnp.clip(
        commit - commit_step * (fixed_cost - dispatch / capacity + w_comm + penalty * (commit - comm_mean)), 0.0, 1.0
    )
    step_gen = 1.0 / (quadratic + penalty + 2.0)
    return commit, jnp.clip(dispatch - step_gen * grad, 0.0, capacity * commit)


def summed(prices, at):
    total = prices[(0, *at)].astype(F32)
    for i in range(1, prices.shape[0]):
        total = total + prices[(i, *at)].astype(F32)
    return total


def first_update(near, far, imbalance, data, same, outside_gen, first, commit_out, dispatch_out, injection):
    shape = dispatch_out.shape[1:]
    for chip in range(data.shape[0]):
        values = data[chip]
        start = jnp.broadcast_to(0.25 * values[3:4], shape)
        half = jnp.full(shape, 0.5, F32)
        commit, dispatch = moved(values, near[chip].astype(F32) + far[chip].astype(F32), imbalance, half, start, 0.0, 0.0, half, start)
        commit_out[chip] = commit
        dispatch_out[chip] = dispatch
        injection[chip] = gen_injection(dispatch, same[chip], outside_gen[chip], first[chip])


def second_update(
    area, near, far, imbalance, data, same, outside_gen, first, commit_in, dispatch_in, weight,
    commit_out, dispatch_out, injection, terms,
):
    rows = dispatch_in.shape[1]
    for chip in range(data.shape[0]):
        values = data[chip]
        start = jnp.broadcast_to(0.25 * values[3:4], dispatch_in.shape[1:])
        half = jnp.full(start.shape, 0.5, F32)
        commit, dispatch = moved(
            values, near[chip].astype(F32) + far[chip].astype(F32), imbalance, commit_in[chip], dispatch_in[chip], 0.0, 0.0, half, start
        )
        injection[chip] = gen_injection(dispatch, same[chip], outside_gen[chip], first[chip])
        commit_out[chip] = commit
        dispatch_out[chip] = dispatch
    own = lax.div(area[0], 2)
    terms[:rows] = weight[:1] * commit_out[own]
    terms[rows : 2 * rows] = weight[:1] * dispatch_out[own]
    terms[2 * rows :] = weight[...]


def add_terms(*refs):
    refs[-1][...] = (refs[0][...] + refs[1][...]) + (refs[2][...] + refs[3][...])


def mean_kernel(weight, terms0, terms1, terms2, terms3, pieces, prob):
    total = (terms0[...] + terms1[...]) + (terms2[...] + terms3[...])
    rows = pieces.shape[1]
    prob[...] = weight[...] / total[2 * rows :]
    for i in range(2):
        mean = total[i * rows : (i + 1) * rows] / total[2 * rows : 2 * rows + 1]
        high = mean.astype(BF16)
        pieces[2 * i] = high
        pieces[2 * i + 1] = (mean - high.astype(F32)).astype(BF16)


def third_update(
    area, near, far, imbalance, data, same, outside_gen, first, commit_in, dispatch_in, state, injection, kept,
):
    chips = data.shape[0]
    for chip in range(chips):
        at = chips + 4 * (chip % 4)
        near_by = lax.div(area[0], 8) == chip // 4
        parts = [jnp.where(near_by, near[at + i].astype(F32), far[at + i].astype(F32)) for i in range(4)]
        comm_mean, disp_mean = parts[0] + parts[1], parts[2] + parts[3]
        commit, dispatch = commit_in[chip], dispatch_in[chip]
        w_comm = penalty * (commit - comm_mean)
        w_disp = penalty * (dispatch - disp_mean)
        commit, dispatch = moved(
            data[chip], near[chip].astype(F32) + far[chip].astype(F32), imbalance, commit, dispatch, w_comm, w_disp, comm_mean, disp_mean
        )
        injection[chip] = gen_injection(dispatch, same[chip], outside_gen[chip], first[chip])
        for i, value in enumerate((commit, dispatch, w_comm, w_disp, comm_mean, disp_mean)):
            kept[i, chip] = value
    own = lax.div(area[0], 2)
    for i in range(6):
        state[i] = kept[i, own]


def last_update(area, prices, imbalance, data, state, prob, dispatch_out, terms):
    commit, dispatch = moved(
        data[lax.div(area[0], 2)], summed(prices, ()), imbalance, *(state[i] for i in range(6))
    )
    dispatch_out[...] = dispatch
    rows = commit.shape[0]
    terms[:rows] = prob[:1] * commit
    terms[rows:] = prob[:1] * dispatch


def last_means(terms0, terms1, terms2, terms3, comm_mean, disp_mean):
    total = (terms0[...] + terms1[...]) + (terms2[...] + terms3[...])
    rows = comm_mean.shape[0]
    comm_mean[...] = total[:rows]
    disp_mean[...] = total[rows:]


def call(kernel, outs, *args, mib=4, cost=1, scalars=0, **more):
    if scalars:
        memories = [pltpu.SMEM] * scalars + [pltpu.VMEM] * (len(args) - scalars)
        more["in_specs"] = [pl.BlockSpec(memory_space=memory) for memory in memories]
    return pl.pallas_call(
        kernel,
        out_shape=[jax.ShapeDtypeStruct(shape, dtype) for shape, dtype in outs],
        compiler_params=pltpu.CompilerParams(vmem_limit_bytes=mib * MIB),
        cost_estimate=pl.CostEstimate(flops=0, transcendentals=0, bytes_accessed=cost * 3_000_000),
        **more,
    )(*args)


def spread(copies, axis, groups=None):
    return lax.all_to_all(copies, axis, split_axis=0, concat_axis=0, tiled=True, axis_index_groups=groups)


def swapped(block, axis, bits):
    return lax.ppermute(block, axis, [(i, i ^ bits) for i in range(lax.axis_size(axis))])


def on_device(wind, load, ptdf_tiles, tile_cols, line_cap, gen_bus, gen_data, prob_weight):
    _, hours, buses = wind.shape
    gens = gen_bus.shape[0]
    lines = line_cap.shape[0]
    areas = lax.axis_size("area")
    scens = lax.axis_size("scen")
    chips = areas // 2
    area = lax.axis_index("area")[None]
    groups = [[2 * i + c for i in range(chips)] for c in range(2)]
    state = (hours, gens)

    [sent] = call(
        prepare_kernel,
        [((chips, 20, hours, 128), BF16)],
        area, wind[0], load, gen_bus[None, :], gen_data,
        mib=56, scalars=1,
    )
    mine = spread(sent, "area", groups)
    other = swapped(mine, "area", 1)
    *params, weight, cols, cap = call(
        params_kernel,
        [
            ((chips, 4, gens), F32),
            ((chips, gens, gens), BF16),
            ((chips, *state), F32),
            ((chips, 1, gens), F32),
            ((8, gens), F32),
            (tile_cols.shape, jnp.int32),
            ((1, lines), F32),
        ],
        prob_weight, mine, tile_cols, line_cap[None, :],
        mib=8, scalars=1,
    )

    def whole(shape):
        return pl.BlockSpec(shape, lambda k: (0,) * len(shape))

    starts = [
        ((areas, lines, gens), BF16),
        ((chips, *state), BF16),
        ((hours, lines), F32),
        ((hours, 128), F32),
        ((hours, 128), F32),
        ((hours, lines), BF16),
    ]
    matrix, partial, base, imb_base, imbalance, excess = call(
        start_kernel,
        starts,
        cols, area, ptdf_tiles, mine, other, cap,
        mib=40, cost=16,
        grid=(ptdf_tiles.shape[0],),
        in_specs=[
            pl.BlockSpec(memory_space=pltpu.SMEM),
            pl.BlockSpec(memory_space=pltpu.SMEM),
            pl.BlockSpec((1, *ptdf_tiles.shape[1:]), lambda k: (k, 0, 0, 0)),
            whole(mine.shape),
            whole(other.shape),
            whole(cap.shape),
        ],
        out_specs=[whole(shape) for shape, _ in starts],
        scratch_shapes=[pltpu.VMEM((areas, 16, hours, 128), BF16), pltpu.VMEM((areas, 1, gens), F32)],
    )

    def all_prices(partial, excess, *more):
        theirs = swapped(partial, "area", 1)
        [ours] = call(own_side_prices, [((chips, *state), F32)], area, excess, matrix, cost=2, scalars=1)
        count = sum(a.shape[0] for a in more)
        [total] = call(both_sides, [((chips + count, *state), BF16)], ours, theirs, *more)
        along_x = [swapped(total, "area", bits) for bits in (2, 4, 6)]
        [total] = call(sum_of_four, [((chips + 4 * count, *state), BF16)], area, total, *along_x, scalars=1)
        return total, swapped(total, "area", 8)

    def flow_and_prices(injection, count):
        theirs = swapped(injection, "area", 1)
        [half] = call(own_side_flow, [((hours, lines), F32)], area, injection, matrix, base, cost=2, scalars=1)
        return call(
            other_side_flow,
            [((count, *state), BF16), ((hours, 128), F32), ((hours, lines), BF16), ((hours, lines), F32)],
            area, half, injection, theirs, matrix, imb_base, cap,
            cost=3, scalars=1,
        )

    def near_sum(terms):
        near = [terms] + [swapped(terms, "scen", bits) for bits in (scens // 2, 1, scens // 2 + 1)]
        [terms] = call(add_terms, [(terms.shape, F32)], *near)
        return terms

    def far_terms(terms):
        return [terms] + [swapped(terms, "scen", bits) for bits in (2, 4, 6)]

    eight = ((chips, *state), F32)
    eights = [eight, eight, ((chips, *state), BF16)]
    commit, dispatch, injection = call(
        first_update,
        eights,
        *all_prices(partial, excess), imbalance, *params,
        mib=8,
    )
    partial, imbalance, excess, _ = flow_and_prices(injection, chips)
    commit, dispatch, injection, terms = call(
        second_update,
        [*eights, ((2 * hours + 8, gens), F32)],
        area, *all_prices(partial, excess), imbalance, *params, commit, dispatch, weight,
        mib=8, scalars=1,
    )
    terms = near_sum(terms)
    partial, imbalance, excess, _ = flow_and_prices(injection, chips)
    partial, excess, terms = lax.optimization_barrier((partial, excess, terms))
    pieces, prob = call(
        mean_kernel,
        [((4, *state), BF16), ((8, gens), F32)],
        weight, *far_terms(terms),
    )
    kept, injection = call(
        third_update,
        [((6, *state), F32), ((chips, *state), BF16)],
        area, *all_prices(partial, excess, pieces), imbalance, *params, commit, dispatch,
        mib=8, scalars=1,
        scratch_shapes=[pltpu.VMEM((6, chips, *state), F32)],
    )
    partial, imbalance, _, flow = flow_and_prices(injection, areas)
    dispatch, terms = call(
        last_update,
        [(state, F32), ((2 * hours, gens), F32)],
        area, spread(partial, "area"), imbalance, params[0], kept, prob,
        scalars=1,
    )
    comm_mean, disp_mean = call(last_means, [(state, F32), (state, F32)], *far_terms(near_sum(terms)))
    return comm_mean, disp_mean, dispatch[None], flow[None]


def solution(mesh):
    placed = (
        P("scen", None, "area"),
        P(None, "area"),
        P("area", None, None, None),
        P("area", None),
        P("area"),
        P("area"),
        P(None, "area"),
        P("scen"),
    )
    return jax.shard_map(
        on_device,
        mesh=mesh,
        in_specs=placed,
        out_specs=(
            P(None, "area"),
            P(None, "area"),
            P("scen", None, "area"),
            P("scen", None, "area"),
        ),
        check_vma=False,
    )
```

```python
import jax
import jax.numpy as jnp
from jax import lax
from jax.experimental import pallas as pl
from jax.experimental.pallas import tpu as pltpu
from jax.sharding import PartitionSpec as P

BUSES = 24576
penalty = 1.0
flow_weight = 0.25
commit_step = 0.5
F32 = jnp.float32
BF16 = jnp.bfloat16
MIB = 1 << 20


def nt(a, b):
    return lax.dot_general(a, b, (((1,), (1,)), ((), ())), preferred_element_type=F32)


def nn(a, b):
    return jnp.dot(a, b, preferred_element_type=F32)


def at_shared_buses(dispatch, same):
    high = dispatch.astype(BF16)
    rest = dispatch - high.astype(F32)
    middle = rest.astype(BF16)
    low = (rest - middle.astype(F32)).astype(BF16)
    return nn(high, same) + (nn(middle, same) + nn(low, same))


def gen_injection(dispatch, same, outside_gen, first):
    placed = at_shared_buses(dispatch, same)
    return jnp.where(first > 0.5, placed + outside_gen, 0.0).astype(BF16)


def first_of(shared):
    gens = shared.shape[0]
    earlier = shared & (
        lax.broadcasted_iota(jnp.int32, (gens, gens), 0) < lax.broadcasted_iota(jnp.int32, (gens, gens), 1)
    )
    return 1.0 - jnp.max(earlier.astype(F32), axis=0, keepdims=True)


def as_column(row):
    return jnp.transpose(jnp.broadcast_to(row, (128, row.shape[1])))[:, :1]


def pieces_of(values):
    high = values.astype(BF16).astype(F32)
    middle = (values - high).astype(BF16).astype(F32)
    return high, middle, values - high - middle


def stacked(lines, rows):
    line = lax.broadcasted_iota(jnp.int32, (rows, lines[0].shape[1]), 0)
    out = jnp.zeros(line.shape, F32)
    for i, values in enumerate(lines):
        out = jnp.where(line == i, values, out)
    return out.astype(BF16)


def prepare_kernel(area, wind, load, bus, data, sent):
    rows, buses = wind.shape
    gens = bus.shape[1]
    row_int = bus[...] - area[0] * buses
    row = row_int.astype(F32)
    col = as_column(row)
    onehot = (col == lax.broadcasted_iota(jnp.int32, (gens, buses), 1).astype(F32)).astype(F32).astype(BF16)
    held = nn(jnp.ones((8, gens), BF16), onehot)[:1]
    wind_gen, load_gen = nt(wind[...], onehot), nt(load[...], onehot)
    shared = col == row
    dispatch = jnp.broadcast_to(0.25 * data[3:4, :], (rows, gens))
    injection = gen_injection(dispatch, shared.astype(F32).astype(BF16), wind_gen - load_gen, first_of(shared))
    base = jnp.where(held > 0.5, 0.0, wind[...].astype(F32) - load[...].astype(F32)).astype(BF16)
    tile_at = row_int // 128
    lane_at = (row_int - 128 * tile_at).astype(F32)
    lines = [tile_at.astype(F32), lane_at]
    for i in range(4):
        lines.extend(pieces_of(data[i : i + 1, :]))
    wind_gen, load_gen = wind_gen.astype(BF16), load_gen.astype(BF16)
    for half in range(2):
        lanes = slice(128 * half, 128 * (half + 1))
        info = stacked([values[:, lanes] for values in lines], rows)
        for copy in range(sent.shape[0]):
            sent[copy, 12 + half] = injection[:, lanes]
            sent[copy, 14 + half] = info
            sent[copy, 16 + half] = wind_gen[:, lanes]
            sent[copy, 18 + half] = load_gen[:, lanes]
    for copy in range(sent.shape[0]):
        for j in range(12):
            sent[copy, j] = base[:, 128 * j : 128 * (j + 1)]


def side_by_side(blocks, *at):
    left, right = blocks[at].astype(F32), blocks[(*at[:-1], at[-1] + 1)].astype(F32)
    return jnp.concatenate([left, right], axis=1)


def params_kernel(prob_weight, mine, cols, cap, data, same, outside_gen, first, weight, cols_out, cap_out):
    cols_out[...] = cols[...]
    cap_out[...] = cap[...]
    weight[...] = jnp.full(weight.shape, prob_weight[0].astype(F32))
    for chip in range(mine.shape[0]):
        info = side_by_side(mine, chip, 14)
        bus = info[0:1] * 128.0 + info[1:2]
        shared = as_column(bus) == bus
        same[chip] = shared.astype(F32).astype(BF16)
        first[chip] = first_of(shared)
        for i in range(4):
            at = 2 + 3 * i
            data[chip, i : i + 1] = info[at : at + 1] + info[at + 1 : at + 2] + info[at + 2 : at + 3]
        outside_gen[chip] = side_by_side(mine, chip, 16) - side_by_side(mine, chip, 18)


def add_flow(total, inject, matrix, area, rows):
    return total + nt(inject, matrix[area, rows, :])


def excess_of(flow, limit):
    return (flow - jnp.clip(flow, -limit, limit)).astype(BF16)


def lane_sum(total):
    return jnp.broadcast_to(jnp.sum(total, axis=1, keepdims=True), (total.shape[0], 128))


def start_kernel(
    cols, area, tiles, mine, other, cap,
    matrix, partial, base, imb_base, imbalance, excess, held, code,
):
    k = pl.program_id(0)
    areas = matrix.shape[0]
    rows = held.shape[2]
    c = lax.rem(area[0], 2)

    @pl.when(k == 0)
    def _():
        for chip in range(areas // 2):
            for j in range(16):
                held[2 * chip + c, j] = mine[chip, j]
                held[2 * chip + 1 - c, j] = other[chip, j]
        total = jnp.zeros((rows, 128), F32)
        gen_total = jnp.zeros((rows, 128), F32)
        for a in range(areas):
            for j in range(12):
                total += held[a, j].astype(F32)
            for j in range(12, 14):
                gen_total += held[a, j].astype(F32)
            info = side_by_side(held, a, 14)
            code[0, a] = info[0:1]
            code[1, a] = info[1:2]
        before = lane_sum(total)
        imb_base[...] = before
        imbalance[...] = before + lane_sum(gen_total)
        matrix[...] = jnp.zeros_like(matrix)

    at_bus = lax.broadcasted_iota(jnp.int32, (128, 256), 0).astype(F32).astype(BF16)
    one, zero = jnp.ones((128, 256), BF16), jnp.zeros((128, 256), BF16)
    here = pl.ds(pl.multiple_of(k * 128, 128), 128)

    total = jnp.zeros((rows, 128), F32)
    for z in range(tiles.shape[1]):
        t = cols[k, z]
        a = t // 12
        j = t - 12 * a
        tile = tiles[0, z]
        total = total + nt(held[a, j], tile)
        bus = jnp.where(code[0, a] == j.astype(F32), code[1, a], 255.0).astype(BF16)
        pick = jnp.where(at_bus == bus, one, zero)
        matrix[a, here, :] = matrix[a, here, :] + nn(tile, pick).astype(BF16)
    base[:, here] = total

    @pl.when(k == pl.num_programs(0) - 1)
    def _():
        over = []
        for b in range(matrix.shape[1] // 256):
            lines = pl.ds(256 * b, 256)
            flow = base[:, lines]
            for a in range(areas):
                inject = jnp.concatenate([held[a, 12], held[a, 13]], axis=1)
                flow = add_flow(flow, inject, matrix, a, lines)
            over.append(excess_of(flow, cap[:, lines]))
        over = jnp.concatenate(over, axis=1)
        excess[...] = over
        for chip in range(areas // 2):
            partial[chip] = nn(over, matrix[2 * chip + 1 - c]).astype(BF16)


def own_side_prices(area, excess, matrix, partial):
    c = lax.rem(area[0], 2)
    for chip in range(partial.shape[0]):
        partial[chip] = nn(excess[...], matrix[2 * chip + c])


def both_sides(mine, other, *more):
    *extra, total = more
    chips = mine.shape[0]
    for chip in range(chips):
        total[chip] = (mine[chip] + other[chip].astype(F32)).astype(BF16)
    for ref in extra:
        for i in range(ref.shape[0]):
            total[chips + i] = ref[i]


def sum_of_four(area, *refs):
    *refs, total = refs
    a, b, c, d = refs
    chips = total.shape[0] if total.shape == a.shape else 2 * len(refs)
    for i in range(chips):
        pairs = (a[i].astype(F32) + b[i].astype(F32)) + (c[i].astype(F32) + d[i].astype(F32))
        total[i] = pairs.astype(BF16)
    count = a.shape[0] - chips
    for bits, ref in enumerate(refs):
        x = lax.bitwise_xor(lax.rem(lax.div(area[0], 2), 4), bits)
        for i in range(count):
            total[chips + count * x + i] = ref[chips + i]


def own_side_flow(area, injection, matrix, base, flow):
    c = lax.rem(area[0], 2)
    for b in range(matrix.shape[1] // 256):
        lines = pl.ds(256 * b, 256)
        total = base[:, lines]
        for chip in range(injection.shape[0]):
            total = add_flow(total, injection[chip], matrix, 2 * chip + c, lines)
        flow[:, lines] = total


def other_side_flow(area, half_flow, mine, other, matrix, imb_base, cap, partial, imbalance, excess, flow):
    c = lax.rem(area[0], 2)
    chips = mine.shape[0]
    over = []
    for b in range(matrix.shape[1] // 256):
        lines = pl.ds(256 * b, 256)
        total = half_flow[:, lines]
        for chip in range(chips):
            total = add_flow(total, other[chip], matrix, 2 * chip + 1 - c, lines)
        flow[:, lines] = total
        over.append(excess_of(total, cap[:, lines]))
    over = jnp.concatenate(over, axis=1)
    excess[...] = over
    if partial.shape[0] == chips:
        for chip in range(chips):
            partial[chip] = nn(over, matrix[2 * chip + 1 - c]).astype(BF16)
    else:
        for a in range(2 * chips):
            partial[a] = nn(over, matrix[a]).astype(BF16)
    total = jnp.zeros(mine.shape[1:], F32)
    for chip in range(chips):
        total += mine[chip].astype(F32) + other[chip].astype(F32)
    imbalance[...] = imb_base[...] + lane_sum(total)


def moved(data, price, imbalance, commit, dispatch, w_comm, w_disp, comm_mean, disp_mean):
    linear, quadratic, fixed_cost, capacity = (data[i : i + 1] for i in range(4))
    grad = (
        linear
        + quadratic * dispatch
        + flow_weight * price
        + imbalance[:, :1] / BUSES
        + w_disp
        + penalty * (dispatch - disp_mean)
    )
    commit = jnp.clip(
        commit - commit_step * (fixed_cost - dispatch / capacity + w_comm + penalty * (commit - comm_mean)), 0.0, 1.0
    )
    step_gen = 1.0 / (quadratic + penalty + 2.0)
    return commit, jnp.clip(dispatch - step_gen * grad, 0.0, capacity * commit)


def summed(prices, at):
    total = prices[(0, *at)].astype(F32)
    for i in range(1, prices.shape[0]):
        total = total + prices[(i, *at)].astype(F32)
    return total


def first_update(near, far, imbalance, data, same, outside_gen, first, commit_out, dispatch_out, injection):
    shape = dispatch_out.shape[1:]
    for chip in range(data.shape[0]):
        values = data[chip]
        start = jnp.broadcast_to(0.25 * values[3:4], shape)
        half = jnp.full(shape, 0.5, F32)
        commit, dispatch = moved(values, near[chip].astype(F32) + far[chip].astype(F32), imbalance, half, start, 0.0, 0.0, half, start)
        commit_out[chip] = commit
        dispatch_out[chip] = dispatch
        injection[chip] = gen_injection(dispatch, same[chip], outside_gen[chip], first[chip])


def second_update(
    area, near, far, imbalance, data, same, outside_gen, first, commit_in, dispatch_in, weight,
    commit_out, dispatch_out, injection, terms,
):
    rows = dispatch_in.shape[1]
    for chip in range(data.shape[0]):
        values = data[chip]
        start = jnp.broadcast_to(0.25 * values[3:4], dispatch_in.shape[1:])
        half = jnp.full(start.shape, 0.5, F32)
        commit, dispatch = moved(
            values, near[chip].astype(F32) + far[chip].astype(F32), imbalance, commit_in[chip], dispatch_in[chip], 0.0, 0.0, half, start
        )
        injection[chip] = gen_injection(dispatch, same[chip], outside_gen[chip], first[chip])
        commit_out[chip] = commit
        dispatch_out[chip] = dispatch
    own = lax.div(area[0], 2)
    terms[:rows] = weight[:1] * (commit_out[own] - 0.5)
    terms[rows : 2 * rows] = weight[:1] * (dispatch_out[own] - 0.25 * data[own][3:4])
    terms[2 * rows :] = weight[...]


def sum_terms(refs):
    a, b, c, d = (ref[...].astype(F32) for ref in refs)
    return (a + b) + (c + d)


def add_terms(*refs):
    refs[-1][...] = sum_terms(refs[:4]).astype(BF16)


def mean_kernel(weight, terms0, terms1, terms2, terms3, pieces, prob):
    total = sum_terms((terms0, terms1, terms2, terms3))
    rows = pieces.shape[1]
    weights = total[2 * rows :]
    prob[...] = weight[...] / weights
    for i in range(2):
        pieces[i] = (total[i * rows : (i + 1) * rows] / weights[:1]).astype(BF16)


def third_update(
    area, near, far, imbalance, data, same, outside_gen, first, commit_in, dispatch_in, state, injection, kept,
):
    chips = data.shape[0]
    for chip in range(chips):
        at = chips + 2 * (chip % 4)
        near_by = lax.div(area[0], 8) == chip // 4
        parts = [jnp.where(near_by, near[at + i].astype(F32), far[at + i].astype(F32)) for i in range(2)]
        comm_mean, disp_mean = 0.5 + parts[0], 0.25 * data[chip][3:4] + parts[1]
        commit, dispatch = commit_in[chip], dispatch_in[chip]
        w_comm = penalty * (commit - comm_mean)
        w_disp = penalty * (dispatch - disp_mean)
        commit, dispatch = moved(
            data[chip], near[chip].astype(F32) + far[chip].astype(F32), imbalance, commit, dispatch, w_comm, w_disp, comm_mean, disp_mean
        )
        injection[chip] = gen_injection(dispatch, same[chip], outside_gen[chip], first[chip])
        for i, value in enumerate((commit, dispatch, w_comm, w_disp, comm_mean, disp_mean)):
            kept[i, chip] = value
    own = lax.div(area[0], 2)
    for i in range(6):
        state[i] = kept[i, own]


def last_update(area, prices, imbalance, data, state, prob, dispatch_out, terms):
    commit, dispatch = moved(
        data[lax.div(area[0], 2)], summed(prices, ()), imbalance, *(state[i] for i in range(6))
    )
    dispatch_out[...] = dispatch
    rows = commit.shape[0]
    terms[:rows] = prob[:1] * (commit - state[4])
    terms[rows:] = prob[:1] * (dispatch - state[5])


def last_means(state, terms0, terms1, terms2, terms3, comm_mean, disp_mean):
    total = sum_terms((terms0, terms1, terms2, terms3))
    rows = comm_mean.shape[0]
    comm_mean[...] = state[4] + total[:rows]
    disp_mean[...] = state[5] + total[rows:]


def call(kernel, outs, *args, mib=4, cost=1, scalars=0, **more):
    if scalars:
        memories = [pltpu.SMEM] * scalars + [pltpu.VMEM] * (len(args) - scalars)
        more["in_specs"] = [pl.BlockSpec(memory_space=memory) for memory in memories]
    return pl.pallas_call(
        kernel,
        out_shape=[jax.ShapeDtypeStruct(shape, dtype) for shape, dtype in outs],
        compiler_params=pltpu.CompilerParams(vmem_limit_bytes=mib * MIB),
        cost_estimate=pl.CostEstimate(flops=0, transcendentals=0, bytes_accessed=cost * 3_000_000),
        **more,
    )(*args)


def spread(copies, axis, groups=None):
    return lax.all_to_all(copies, axis, split_axis=0, concat_axis=0, tiled=True, axis_index_groups=groups)


def swapped(block, axis, bits):
    return lax.ppermute(block, axis, [(i, i ^ bits) for i in range(lax.axis_size(axis))])


def on_device(wind, load, ptdf_tiles, tile_cols, line_cap, gen_bus, gen_data, prob_weight):
    _, hours, buses = wind.shape
    gens = gen_bus.shape[0]
    lines = line_cap.shape[0]
    areas = lax.axis_size("area")
    scens = lax.axis_size("scen")
    chips = areas // 2
    area = lax.axis_index("area")[None]
    groups = [[2 * i + c for i in range(chips)] for c in range(2)]
    state = (hours, gens)

    [sent] = call(
        prepare_kernel,
        [((chips, 20, hours, 128), BF16)],
        area, wind[0], load, gen_bus[None, :], gen_data,
        mib=56, scalars=1,
    )
    mine = spread(sent, "area", groups)
    other = swapped(mine, "area", 1)
    *params, weight, cols, cap = call(
        params_kernel,
        [
            ((chips, 4, gens), F32),
            ((chips, gens, gens), BF16),
            ((chips, *state), F32),
            ((chips, 1, gens), F32),
            ((8, gens), F32),
            (tile_cols.shape, jnp.int32),
            ((1, lines), F32),
        ],
        prob_weight, mine, tile_cols, line_cap[None, :],
        mib=8, scalars=1,
    )

    def whole(shape):
        return pl.BlockSpec(shape, lambda k: (0,) * len(shape))

    starts = [
        ((areas, lines, gens), BF16),
        ((chips, *state), BF16),
        ((hours, lines), F32),
        ((hours, 128), F32),
        ((hours, 128), F32),
        ((hours, lines), BF16),
    ]
    matrix, partial, base, imb_base, imbalance, excess = call(
        start_kernel,
        starts,
        cols, area, ptdf_tiles, mine, other, cap,
        mib=40, cost=16,
        grid=(ptdf_tiles.shape[0],),
        in_specs=[
            pl.BlockSpec(memory_space=pltpu.SMEM),
            pl.BlockSpec(memory_space=pltpu.SMEM),
            pl.BlockSpec((1, *ptdf_tiles.shape[1:]), lambda k: (k, 0, 0, 0)),
            whole(mine.shape),
            whole(other.shape),
            whole(cap.shape),
        ],
        out_specs=[whole(shape) for shape, _ in starts],
        scratch_shapes=[pltpu.VMEM((areas, 16, hours, 128), BF16), pltpu.VMEM((2, areas, 1, gens), F32)],
    )

    def all_prices(partial, excess, *more):
        theirs = swapped(partial, "area", 1)
        [ours] = call(own_side_prices, [((chips, *state), F32)], area, excess, matrix, cost=2, scalars=1)
        count = sum(a.shape[0] for a in more)
        [total] = call(both_sides, [((chips + count, *state), BF16)], ours, theirs, *more)
        along_x = [swapped(total, "area", bits) for bits in (2, 4, 6)]
        [total] = call(sum_of_four, [((chips + 4 * count, *state), BF16)], area, total, *along_x, scalars=1)
        return total, swapped(total, "area", 8)

    def flow_and_prices(injection, count):
        theirs = swapped(injection, "area", 1)
        [half] = call(own_side_flow, [((hours, lines), F32)], area, injection, matrix, base, cost=2, scalars=1)
        return call(
            other_side_flow,
            [((count, *state), BF16), ((hours, 128), F32), ((hours, lines), BF16), ((hours, lines), F32)],
            area, half, injection, theirs, matrix, imb_base, cap,
            cost=3, scalars=1,
        )

    def near_sum(terms):
        near = [terms] + [swapped(terms, "scen", bits) for bits in (scens // 2, 1, scens // 2 + 1)]
        [terms] = call(add_terms, [(terms.shape, BF16)], *near)
        return terms

    def far_terms(terms):
        return [terms] + [swapped(terms, "scen", bits) for bits in (2, 4, 6)]

    eight = ((chips, *state), F32)
    eights = [eight, eight, ((chips, *state), BF16)]
    commit, dispatch, injection = call(
        first_update,
        eights,
        *all_prices(partial, excess), imbalance, *params,
        mib=8,
    )
    partial, imbalance, excess, _ = flow_and_prices(injection, chips)
    commit, dispatch, injection, terms = call(
        second_update,
        [*eights, ((2 * hours + 8, gens), F32)],
        area, *all_prices(partial, excess), imbalance, *params, commit, dispatch, weight,
        mib=8, scalars=1,
    )
    terms = near_sum(terms)
    partial, imbalance, excess, _ = flow_and_prices(injection, chips)
    partial, excess, terms = lax.optimization_barrier((partial, excess, terms))
    pieces, prob = call(
        mean_kernel,
        [((2, *state), BF16), ((8, gens), F32)],
        weight, *far_terms(terms),
    )
    kept, injection = call(
        third_update,
        [((6, *state), F32), ((chips, *state), BF16)],
        area, *all_prices(partial, excess, pieces), imbalance, *params, commit, dispatch,
        mib=8, scalars=1,
        scratch_shapes=[pltpu.VMEM((6, chips, *state), F32)],
    )
    partial, imbalance, _, flow = flow_and_prices(injection, areas)
    dispatch, terms = call(
        last_update,
        [(state, F32), ((2 * hours, gens), F32)],
        area, spread(partial, "area"), imbalance, params[0], kept, prob,
        scalars=1,
    )
    comm_mean, disp_mean = call(last_means, [(state, F32), (state, F32)], kept, *far_terms(near_sum(terms)))
    return comm_mean, disp_mean, dispatch[None], flow[None]


def solution(mesh):
    placed = (
        P("scen", None, "area"),
        P(None, "area"),
        P("area", None, None, None),
        P("area", None),
        P("area"),
        P("area"),
        P(None, "area"),
        P("scen"),
    )
    return jax.shard_map(
        on_device,
        mesh=mesh,
        in_specs=placed,
        out_specs=(
            P(None, "area"),
            P(None, "area"),
            P("scen", None, "area"),
            P("scen", None, "area"),
        ),
        check_vma=False,
    )
```

```python
import jax
import jax.numpy as jnp
from jax import lax
from jax.experimental import pallas as pl
from jax.experimental.pallas import tpu as pltpu
from jax.sharding import PartitionSpec as P

BUSES = 24576
penalty = 1.0
flow_weight = 0.25
commit_step = 0.5
F32 = jnp.float32
BF16 = jnp.bfloat16
MIB = 1 << 20


def nt(a, b):
    return lax.dot_general(a, b, (((1,), (1,)), ((), ())), preferred_element_type=F32)


def nn(a, b):
    return jnp.dot(a, b, preferred_element_type=F32)


def at_shared_buses(dispatch, same):
    high = dispatch.astype(BF16)
    rest = dispatch - high.astype(F32)
    middle = rest.astype(BF16)
    low = (rest - middle.astype(F32)).astype(BF16)
    return nn(high, same) + (nn(middle, same) + nn(low, same))


def gen_injection(dispatch, same, outside_gen, first):
    placed = at_shared_buses(dispatch, same)
    return jnp.where(first > 0.5, placed + outside_gen, 0.0).astype(BF16)


def first_of(shared):
    gens = shared.shape[0]
    earlier = shared & (
        lax.broadcasted_iota(jnp.int32, (gens, gens), 0) < lax.broadcasted_iota(jnp.int32, (gens, gens), 1)
    )
    return 1.0 - jnp.max(earlier.astype(F32), axis=0, keepdims=True)


def as_column(row):
    return jnp.transpose(jnp.broadcast_to(row, (128, row.shape[1])))[:, :1]


def pieces_of(values):
    high = values.astype(BF16).astype(F32)
    middle = (values - high).astype(BF16).astype(F32)
    return high, middle, values - high - middle


def stacked(lines, rows):
    line = lax.broadcasted_iota(jnp.int32, (rows, lines[0].shape[1]), 0)
    out = jnp.zeros(line.shape, F32)
    for i, values in enumerate(lines):
        out = jnp.where(line == i, values, out)
    return out.astype(BF16)


def prepare_kernel(area, wind, load, bus, data, sent):
    rows, buses = wind.shape
    gens = bus.shape[1]
    row_int = bus[...] - area[0] * buses
    row = row_int.astype(F32)
    col = as_column(row)
    onehot = (col == lax.broadcasted_iota(jnp.int32, (gens, buses), 1).astype(F32)).astype(F32).astype(BF16)
    held = nn(jnp.ones((8, gens), BF16), onehot)[:1]
    wind_gen, load_gen = nt(wind[...], onehot), nt(load[...], onehot)
    shared = col == row
    dispatch = jnp.broadcast_to(0.25 * data[3:4, :], (rows, gens))
    injection = gen_injection(dispatch, shared.astype(F32).astype(BF16), wind_gen - load_gen, first_of(shared))
    base = jnp.where(held > 0.5, 0.0, wind[...].astype(F32) - load[...].astype(F32)).astype(BF16)
    tile_at = row_int // 128
    lane_at = (row_int - 128 * tile_at).astype(F32)
    lines = [tile_at.astype(F32), lane_at]
    for i in range(4):
        lines.extend(pieces_of(data[i : i + 1, :]))
    wind_gen, load_gen = wind_gen.astype(BF16), load_gen.astype(BF16)
    for half in range(2):
        lanes = slice(128 * half, 128 * (half + 1))
        info = stacked([values[:, lanes] for values in lines], rows)
        for copy in range(sent.shape[0]):
            sent[copy, 12 + half] = injection[:, lanes]
            sent[copy, 14 + half] = info
            sent[copy, 16 + half] = wind_gen[:, lanes]
            sent[copy, 18 + half] = load_gen[:, lanes]
    for copy in range(sent.shape[0]):
        for j in range(12):
            sent[copy, j] = base[:, 128 * j : 128 * (j + 1)]


def side_by_side(blocks, *at):
    left, right = blocks[at].astype(F32), blocks[(*at[:-1], at[-1] + 1)].astype(F32)
    return jnp.concatenate([left, right], axis=1)


def params_kernel(prob_weight, mine, cols, cap, data, same, outside_gen, first, weight, cols_out, cap_out):
    cols_out[...] = cols[...]
    cap_out[...] = cap[...]
    weight[...] = jnp.full(weight.shape, prob_weight[0].astype(F32))
    for chip in range(mine.shape[0]):
        info = side_by_side(mine, chip, 14)
        bus = info[0:1] * 128.0 + info[1:2]
        shared = as_column(bus) == bus
        same[chip] = shared.astype(F32).astype(BF16)
        first[chip] = first_of(shared)
        for i in range(4):
            at = 2 + 3 * i
            data[chip, i : i + 1] = info[at : at + 1] + info[at + 1 : at + 2] + info[at + 2 : at + 3]
        outside_gen[chip] = side_by_side(mine, chip, 16) - side_by_side(mine, chip, 18)


def add_flow(total, inject, matrix, area, rows):
    return total + nt(inject, matrix[area, rows, :])


def excess_of(flow, limit):
    return (flow - jnp.clip(flow, -limit, limit)).astype(BF16)


def lane_sum(total):
    return jnp.broadcast_to(jnp.sum(total, axis=1, keepdims=True), (total.shape[0], 128))


def start_kernel(
    cols, area, tiles, mine, other, cap,
    matrix, partial, base, imb_base, imbalance, excess, held, code,
):
    k = pl.program_id(0)
    areas = matrix.shape[0]
    rows = held.shape[2]
    c = lax.rem(area[0], 2)

    @pl.when(k == 0)
    def _():
        for chip in range(areas // 2):
            for j in range(16):
                held[2 * chip + c, j] = mine[chip, j]
                held[2 * chip + 1 - c, j] = other[chip, j]
        total = jnp.zeros((rows, 128), F32)
        gen_total = jnp.zeros((rows, 128), F32)
        for a in range(areas):
            for j in range(12):
                total += held[a, j].astype(F32)
            for j in range(12, 14):
                gen_total += held[a, j].astype(F32)
            info = side_by_side(held, a, 14)
            code[0, a] = info[0:1]
            code[1, a] = info[1:2]
        before = lane_sum(total)
        imb_base[...] = before
        imbalance[...] = before + lane_sum(gen_total)
        matrix[...] = jnp.zeros_like(matrix)

    at_bus = lax.broadcasted_iota(jnp.int32, (128, 256), 0).astype(F32).astype(BF16)
    one, zero = jnp.ones((128, 256), BF16), jnp.zeros((128, 256), BF16)
    here = pl.ds(pl.multiple_of(k * 128, 128), 128)

    total = jnp.zeros((rows, 128), F32)
    for z in range(tiles.shape[1]):
        t = cols[k, z]
        a = t // 12
        j = t - 12 * a
        tile = tiles[0, z]
        total = total + nt(held[a, j], tile)
        bus = jnp.where(code[0, a] == j.astype(F32), code[1, a], 255.0).astype(BF16)
        pick = jnp.where(at_bus == bus, one, zero)
        matrix[a, here, :] = matrix[a, here, :] + nn(tile, pick).astype(BF16)
    base[:, here] = total

    @pl.when(k == pl.num_programs(0) - 1)
    def _():
        over = []
        for b in range(matrix.shape[1] // 256):
            lines = pl.ds(256 * b, 256)
            flow = base[:, lines]
            for a in range(areas):
                inject = jnp.concatenate([held[a, 12], held[a, 13]], axis=1)
                flow = add_flow(flow, inject, matrix, a, lines)
            over.append(excess_of(flow, cap[:, lines]))
        over = jnp.concatenate(over, axis=1)
        excess[...] = over
        for chip in range(areas // 2):
            partial[chip] = nn(over, matrix[2 * chip + 1 - c]).astype(BF16)


def own_side_prices(area, excess, matrix, partial):
    c = lax.rem(area[0], 2)
    for chip in range(partial.shape[0]):
        partial[chip] = nn(excess[...], matrix[2 * chip + c])


def both_sides(mine, other, *more):
    *extra, total = more
    chips = mine.shape[0]
    for chip in range(chips):
        total[chip] = (mine[chip] + other[chip].astype(F32)).astype(BF16)
    for ref in extra:
        for i in range(ref.shape[0]):
            total[chips + i] = ref[i]


def sum_of_four(area, *refs):
    *refs, total = refs
    a, b, c, d = refs
    chips = total.shape[0] if total.shape == a.shape else 2 * len(refs)
    for i in range(chips):
        pairs = (a[i].astype(F32) + b[i].astype(F32)) + (c[i].astype(F32) + d[i].astype(F32))
        total[i] = pairs.astype(BF16)
    count = a.shape[0] - chips
    for bits, ref in enumerate(refs):
        x = lax.bitwise_xor(lax.rem(lax.div(area[0], 2), 4), bits)
        for i in range(count):
            total[chips + count * x + i] = ref[chips + i]


def own_side_flow(area, injection, matrix, base, flow):
    c = lax.rem(area[0], 2)
    for b in range(matrix.shape[1] // 256):
        lines = pl.ds(256 * b, 256)
        total = base[:, lines]
        for chip in range(injection.shape[0]):
            total = add_flow(total, injection[chip], matrix, 2 * chip + c, lines)
        flow[:, lines] = total


def other_side_flow(area, half_flow, mine, other, matrix, imb_base, cap, partial, imbalance, excess, flow):
    c = lax.rem(area[0], 2)
    chips = mine.shape[0]
    over = []
    for b in range(matrix.shape[1] // 256):
        lines = pl.ds(256 * b, 256)
        total = half_flow[:, lines]
        for chip in range(chips):
            total = add_flow(total, other[chip], matrix, 2 * chip + 1 - c, lines)
        flow[:, lines] = total
        over.append(excess_of(total, cap[:, lines]))
    over = jnp.concatenate(over, axis=1)
    excess[...] = over
    if partial.shape[0] == chips:
        for chip in range(chips):
            partial[chip] = nn(over, matrix[2 * chip + 1 - c]).astype(BF16)
    else:
        for a in range(2 * chips):
            partial[a] = nn(over, matrix[a]).astype(BF16)
    total = jnp.zeros(mine.shape[1:], F32)
    for chip in range(chips):
        total += mine[chip].astype(F32) + other[chip].astype(F32)
    imbalance[...] = imb_base[...] + lane_sum(total)


def moved(data, price, imbalance, commit, dispatch, w_comm, w_disp, comm_mean, disp_mean):
    linear, quadratic, fixed_cost, capacity = (data[i : i + 1] for i in range(4))
    grad = (
        linear
        + quadratic * dispatch
        + flow_weight * price
        + imbalance[:, :1] / BUSES
        + w_disp
        + penalty * (dispatch - disp_mean)
    )
    commit = jnp.clip(
        commit - commit_step * (fixed_cost - dispatch / capacity + w_comm + penalty * (commit - comm_mean)), 0.0, 1.0
    )
    step_gen = 1.0 / (quadratic + penalty + 2.0)
    return commit, jnp.clip(dispatch - step_gen * grad, 0.0, capacity * commit)


def summed(prices, at):
    total = prices[(0, *at)].astype(F32)
    for i in range(1, prices.shape[0]):
        total = total + prices[(i, *at)].astype(F32)
    return total


def first_update(near, far, imbalance, data, same, outside_gen, first, commit_out, dispatch_out, injection):
    shape = dispatch_out.shape[1:]
    for chip in range(data.shape[0]):
        values = data[chip]
        start = jnp.broadcast_to(0.25 * values[3:4], shape)
        half = jnp.full(shape, 0.5, F32)
        commit, dispatch = moved(values, near[chip].astype(F32) + far[chip].astype(F32), imbalance, half, start, 0.0, 0.0, half, start)
        commit_out[chip] = commit
        dispatch_out[chip] = dispatch
        injection[chip] = gen_injection(dispatch, same[chip], outside_gen[chip], first[chip])


def second_update(
    area, near, far, imbalance, data, same, outside_gen, first, commit_in, dispatch_in, weight,
    commit_out, dispatch_out, injection, terms, change,
):
    rows = dispatch_in.shape[1]
    for chip in range(data.shape[0]):
        values = data[chip]
        start = jnp.broadcast_to(0.25 * values[3:4], dispatch_in.shape[1:])
        half = jnp.full(start.shape, 0.5, F32)
        commit, dispatch = moved(
            values, near[chip].astype(F32) + far[chip].astype(F32), imbalance, commit_in[chip], dispatch_in[chip], 0.0, 0.0, half, start
        )
        injection[chip] = gen_injection(dispatch, same[chip], outside_gen[chip], first[chip])
        commit_out[chip] = commit
        dispatch_out[chip] = dispatch
    own = lax.div(area[0], 2)
    moves = commit_out[own] - 0.5, dispatch_out[own] - 0.25 * data[own][3:4]
    for i, move in enumerate(moves):
        change[i] = move
        terms[i * rows : (i + 1) * rows] = weight[:1] * move
    terms[2 * rows :] = weight[...]


def sum_terms(refs):
    a, b, c, d = (ref[...].astype(F32) for ref in refs)
    return (a + b) + (c + d)


def add_terms(*refs):
    total = sum_terms(refs[:4])
    for ref in refs[4:]:
        ref[...] = total.astype(ref.dtype)


def mean_kernel(weight, change, terms0, terms1, terms2, terms3, apart, prob):
    total = sum_terms((terms0, terms1, terms2, terms3))
    rows = apart.shape[1]
    weights = total[2 * rows :]
    prob[...] = weight[...] / weights
    for i in range(2):
        apart[i] = (change[i] - total[i * rows : (i + 1) * rows] / weights[:1]).astype(BF16)


def third_update(
    area, near, far, imbalance, data, same, outside_gen, first, commit_in, dispatch_in, state, injection, kept,
):
    chips = data.shape[0]
    for chip in range(chips):
        at = chips + 2 * (chip % 4)
        near_by = lax.div(area[0], 8) == chip // 4
        parts = [jnp.where(near_by, near[at + i].astype(F32), far[at + i].astype(F32)) for i in range(2)]
        commit, dispatch = commit_in[chip], dispatch_in[chip]
        comm_mean, disp_mean = commit - parts[0], dispatch - parts[1]
        w_comm = penalty * parts[0]
        w_disp = penalty * parts[1]
        commit, dispatch = moved(
            data[chip], near[chip].astype(F32) + far[chip].astype(F32), imbalance, commit, dispatch, w_comm, w_disp, comm_mean, disp_mean
        )
        injection[chip] = gen_injection(dispatch, same[chip], outside_gen[chip], first[chip])
        for i, value in enumerate((commit, dispatch, w_comm, w_disp, comm_mean, disp_mean)):
            kept[i, chip] = value
    own = lax.div(area[0], 2)
    for i in range(6):
        state[i] = kept[i, own]


def last_update(area, prices, imbalance, data, state, prob, dispatch_out, terms):
    commit, dispatch = moved(
        data[lax.div(area[0], 2)], summed(prices, ()), imbalance, *(state[i] for i in range(6))
    )
    dispatch_out[...] = dispatch
    rows = commit.shape[0]
    terms[:rows] = prob[:1] * commit
    terms[rows:] = prob[:1] * dispatch


def last_means(terms0, terms1, terms2, terms3, comm_mean, disp_mean):
    total = sum_terms((terms0, terms1, terms2, terms3))
    rows = comm_mean.shape[0]
    comm_mean[...] = total[:rows]
    disp_mean[...] = total[rows:]


def call(kernel, outs, *args, mib=4, cost=1, scalars=0, **more):
    if scalars:
        memories = [pltpu.SMEM] * scalars + [pltpu.VMEM] * (len(args) - scalars)
        more["in_specs"] = [pl.BlockSpec(memory_space=memory) for memory in memories]
    return pl.pallas_call(
        kernel,
        out_shape=[jax.ShapeDtypeStruct(shape, dtype) for shape, dtype in outs],
        compiler_params=pltpu.CompilerParams(vmem_limit_bytes=mib * MIB),
        cost_estimate=pl.CostEstimate(flops=0, transcendentals=0, bytes_accessed=cost * 3_000_000),
        **more,
    )(*args)


def spread(copies, axis, groups=None):
    return lax.all_to_all(copies, axis, split_axis=0, concat_axis=0, tiled=True, axis_index_groups=groups)


def swapped(block, axis, bits):
    return lax.ppermute(block, axis, [(i, i ^ bits) for i in range(lax.axis_size(axis))])


def on_device(wind, load, ptdf_tiles, tile_cols, line_cap, gen_bus, gen_data, prob_weight):
    _, hours, buses = wind.shape
    gens = gen_bus.shape[0]
    lines = line_cap.shape[0]
    areas = lax.axis_size("area")
    scens = lax.axis_size("scen")
    chips = areas // 2
    area = lax.axis_index("area")[None]
    groups = [[2 * i + c for i in range(chips)] for c in range(2)]
    state = (hours, gens)

    [sent] = call(
        prepare_kernel,
        [((chips, 20, hours, 128), BF16)],
        area, wind[0], load, gen_bus[None, :], gen_data,
        mib=56, scalars=1,
    )
    mine = spread(sent, "area", groups)
    other = swapped(mine, "area", 1)
    *params, weight, cols, cap = call(
        params_kernel,
        [
            ((chips, 4, gens), F32),
            ((chips, gens, gens), BF16),
            ((chips, *state), F32),
            ((chips, 1, gens), F32),
            ((8, gens), F32),
            (tile_cols.shape, jnp.int32),
            ((1, lines), F32),
        ],
        prob_weight, mine, tile_cols, line_cap[None, :],
        mib=8, scalars=1,
    )

    def whole(shape):
        return pl.BlockSpec(shape, lambda k: (0,) * len(shape))

    starts = [
        ((areas, lines, gens), BF16),
        ((chips, *state), BF16),
        ((hours, lines), F32),
        ((hours, 128), F32),
        ((hours, 128), F32),
        ((hours, lines), BF16),
    ]
    matrix, partial, base, imb_base, imbalance, excess = call(
        start_kernel,
        starts,
        cols, area, ptdf_tiles, mine, other, cap,
        mib=40, cost=16,
        grid=(ptdf_tiles.shape[0],),
        in_specs=[
            pl.BlockSpec(memory_space=pltpu.SMEM),
            pl.BlockSpec(memory_space=pltpu.SMEM),
            pl.BlockSpec((1, *ptdf_tiles.shape[1:]), lambda k: (k, 0, 0, 0)),
            whole(mine.shape),
            whole(other.shape),
            whole(cap.shape),
        ],
        out_specs=[whole(shape) for shape, _ in starts],
        scratch_shapes=[pltpu.VMEM((areas, 16, hours, 128), BF16), pltpu.VMEM((2, areas, 1, gens), F32)],
    )

    def all_prices(partial, excess, *more):
        theirs = swapped(partial, "area", 1)
        [ours] = call(own_side_prices, [((chips, *state), F32)], area, excess, matrix, cost=2, scalars=1)
        count = sum(a.shape[0] for a in more)
        [total] = call(both_sides, [((chips + count, *state), BF16)], ours, theirs, *more)
        along_x = [swapped(total, "area", bits) for bits in (2, 4, 6)]
        [total] = call(sum_of_four, [((chips + 4 * count, *state), BF16)], area, total, *along_x, scalars=1)
        return total, swapped(total, "area", 8)

    def flow_and_prices(injection, count):
        theirs = swapped(injection, "area", 1)
        [half] = call(own_side_flow, [((hours, lines), F32)], area, injection, matrix, base, cost=2, scalars=1)
        return call(
            other_side_flow,
            [((count, *state), BF16), ((hours, 128), F32), ((hours, lines), BF16), ((hours, lines), F32)],
            area, half, injection, theirs, matrix, imb_base, cap,
            cost=3, scalars=1,
        )

    def near_sum(terms, *dtypes):
        near = [terms] + [swapped(terms, "scen", bits) for bits in (scens // 2, 1, scens // 2 + 1)]
        return call(add_terms, [(terms.shape, dtype) for dtype in dtypes], *near)

    def far_terms(terms):
        return [swapped(terms, "scen", bits) for bits in (2, 4, 6)]

    eight = ((chips, *state), F32)
    eights = [eight, eight, ((chips, *state), BF16)]
    commit, dispatch, injection = call(
        first_update,
        eights,
        *all_prices(partial, excess), imbalance, *params,
        mib=8,
    )
    partial, imbalance, excess, _ = flow_and_prices(injection, chips)
    commit, dispatch, injection, terms, change = call(
        second_update,
        [*eights, ((2 * hours + 8, gens), F32), ((2, *state), F32)],
        area, *all_prices(partial, excess), imbalance, *params, commit, dispatch, weight,
        mib=8, scalars=1,
    )
    near, terms = near_sum(terms, F32, BF16)
    partial, imbalance, excess, _ = flow_and_prices(injection, chips)
    partial, excess, terms = lax.optimization_barrier((partial, excess, terms))
    apart, prob = call(
        mean_kernel,
        [((2, *state), BF16), ((8, gens), F32)],
        weight, change, near, *far_terms(terms),
    )
    kept, injection = call(
        third_update,
        [((6, *state), F32), ((chips, *state), BF16)],
        area, *all_prices(partial, excess, apart), imbalance, *params, commit, dispatch,
        mib=8, scalars=1,
        scratch_shapes=[pltpu.VMEM((6, chips, *state), F32)],
    )
    partial, imbalance, _, flow = flow_and_prices(injection, areas)
    dispatch, terms = call(
        last_update,
        [(state, F32), ((2 * hours, gens), F32)],
        area, spread(partial, "area"), imbalance, params[0], kept, prob,
        scalars=1,
    )
    [terms] = near_sum(terms, F32)
    comm_mean, disp_mean = call(last_means, [(state, F32), (state, F32)], terms, *far_terms(terms))
    return comm_mean, disp_mean, dispatch[None], flow[None]


def solution(mesh):
    placed = (
        P("scen", None, "area"),
        P(None, "area"),
        P("area", None, None, None),
        P("area", None),
        P("area"),
        P("area"),
        P(None, "area"),
        P("scen"),
    )
    return jax.shard_map(
        on_device,
        mesh=mesh,
        in_specs=placed,
        out_specs=(
            P(None, "area"),
            P(None, "area"),
            P("scen", None, "area"),
            P("scen", None, "area"),
        ),
        check_vma=False,
    )
```

```python
import jax
import jax.numpy as jnp
from jax import lax
from jax.experimental import pallas as pl
from jax.experimental.pallas import tpu as pltpu
from jax.sharding import PartitionSpec as P

BUSES = 24576
penalty = 1.0
flow_weight = 0.25
commit_step = 0.5
F32 = jnp.float32
BF16 = jnp.bfloat16
MIB = 1 << 20


def nt(a, b):
    return lax.dot_general(a, b, (((1,), (1,)), ((), ())), preferred_element_type=F32)


def nn(a, b):
    return jnp.dot(a, b, preferred_element_type=F32)


def at_shared_buses(dispatch, same):
    high = dispatch.astype(BF16)
    rest = dispatch - high.astype(F32)
    middle = rest.astype(BF16)
    low = (rest - middle.astype(F32)).astype(BF16)
    return nn(high, same) + (nn(middle, same) + nn(low, same))


def gen_injection(dispatch, same, outside_gen, first):
    placed = at_shared_buses(dispatch, same)
    return jnp.where(first > 0.5, placed + outside_gen, 0.0).astype(BF16)


def first_of(shared):
    gens = shared.shape[0]
    earlier = shared & (
        lax.broadcasted_iota(jnp.int32, (gens, gens), 0) < lax.broadcasted_iota(jnp.int32, (gens, gens), 1)
    )
    return 1.0 - jnp.max(earlier.astype(F32), axis=0, keepdims=True)


def as_column(row):
    return jnp.transpose(jnp.broadcast_to(row, (128, row.shape[1])))[:, :1]


def pieces_of(values):
    high = values.astype(BF16).astype(F32)
    middle = (values - high).astype(BF16).astype(F32)
    return high, middle, values - high - middle


def stacked(lines, rows):
    line = lax.broadcasted_iota(jnp.int32, (rows, lines[0].shape[1]), 0)
    out = jnp.zeros(line.shape, F32)
    for i, values in enumerate(lines):
        out = jnp.where(line == i, values, out)
    return out.astype(BF16)


def prepare_kernel(area, wind, load, bus, data, sent):
    rows, buses = wind.shape
    gens = bus.shape[1]
    row_int = bus[...] - area[0] * buses
    row = row_int.astype(F32)
    col = as_column(row)
    onehot = (col == lax.broadcasted_iota(jnp.int32, (gens, buses), 1).astype(F32)).astype(F32).astype(BF16)
    held = nn(jnp.ones((8, gens), BF16), onehot)[:1]
    wind_gen, load_gen = nt(wind[...], onehot), nt(load[...], onehot)
    shared = col == row
    dispatch = jnp.broadcast_to(0.25 * data[3:4, :], (rows, gens))
    injection = gen_injection(dispatch, shared.astype(F32).astype(BF16), wind_gen - load_gen, first_of(shared))
    base = jnp.where(held > 0.5, 0.0, wind[...].astype(F32) - load[...].astype(F32)).astype(BF16)
    tile_at = row_int // 128
    lane_at = (row_int - 128 * tile_at).astype(F32)
    lines = [tile_at.astype(F32), lane_at]
    for i in range(4):
        lines.extend(pieces_of(data[i : i + 1, :]))
    wind_gen, load_gen = wind_gen.astype(BF16), load_gen.astype(BF16)
    for half in range(2):
        lanes = slice(128 * half, 128 * (half + 1))
        info = stacked([values[:, lanes] for values in lines], rows)
        for copy in range(sent.shape[0]):
            sent[copy, 12 + half] = injection[:, lanes]
            sent[copy, 14 + half] = info
            sent[copy, 16 + half] = wind_gen[:, lanes]
            sent[copy, 18 + half] = load_gen[:, lanes]
    for copy in range(sent.shape[0]):
        for j in range(12):
            sent[copy, j] = base[:, 128 * j : 128 * (j + 1)]


def side_by_side(blocks, *at):
    left, right = blocks[at].astype(F32), blocks[(*at[:-1], at[-1] + 1)].astype(F32)
    return jnp.concatenate([left, right], axis=1)


def params_kernel(prob_weight, mine, cols, cap, data, same, outside_gen, first, weight, cols_out, cap_out):
    cols_out[...] = cols[...]
    cap_out[...] = cap[...]
    weight[...] = jnp.full(weight.shape, prob_weight[0].astype(F32))
    for chip in range(mine.shape[0]):
        info = side_by_side(mine, chip, 14)
        bus = info[0:1] * 128.0 + info[1:2]
        shared = as_column(bus) == bus
        same[chip] = shared.astype(F32).astype(BF16)
        first[chip] = first_of(shared)
        for i in range(4):
            at = 2 + 3 * i
            data[chip, i : i + 1] = info[at : at + 1] + info[at + 1 : at + 2] + info[at + 2 : at + 3]
        outside_gen[chip] = side_by_side(mine, chip, 16) - side_by_side(mine, chip, 18)


def add_flow(total, inject, matrix, area, rows):
    return total + nt(inject, matrix[area, rows, :])


def excess_of(flow, limit):
    return (flow - jnp.clip(flow, -limit, limit)).astype(BF16)


def lane_sum(total):
    return jnp.broadcast_to(jnp.sum(total, axis=1, keepdims=True), (total.shape[0], 128))


def start_kernel(
    cols, area, tiles, mine, other, cap,
    matrix, partial, base, imb_base, imbalance, excess, held, code,
):
    k = pl.program_id(0)
    areas = matrix.shape[0]
    rows = held.shape[2]
    c = lax.rem(area[0], 2)

    @pl.when(k == 0)
    def _():
        for chip in range(areas // 2):
            for j in range(16):
                held[2 * chip + c, j] = mine[chip, j]
                held[2 * chip + 1 - c, j] = other[chip, j]
        total = jnp.zeros((rows, 128), F32)
        gen_total = jnp.zeros((rows, 128), F32)
        for a in range(areas):
            for j in range(12):
                total += held[a, j].astype(F32)
            for j in range(12, 14):
                gen_total += held[a, j].astype(F32)
            info = side_by_side(held, a, 14)
            code[0, a] = info[0:1]
            code[1, a] = info[1:2]
        before = lane_sum(total)
        imb_base[...] = before
        imbalance[...] = before + lane_sum(gen_total)
        matrix[...] = jnp.zeros_like(matrix)

    at_bus = lax.broadcasted_iota(jnp.int32, (128, 256), 0).astype(F32).astype(BF16)
    one, zero = jnp.ones((128, 256), BF16), jnp.zeros((128, 256), BF16)
    here = pl.ds(pl.multiple_of(k * 128, 128), 128)

    total = jnp.zeros((rows, 128), F32)
    for z in range(0, tiles.shape[1], 2):
        pair = []
        for slot in (z, z + 1):
            t = cols[k, slot]
            a = t // 12
            j = t - 12 * a
            tile = tiles[0, slot]
            pair.append((held[a, j], tile))
            bus = jnp.where(code[0, a] == j.astype(F32), code[1, a], 255.0).astype(BF16)
            pick = jnp.where(at_bus == bus, one, zero)
            matrix[a, here, :] = matrix[a, here, :] + nn(tile, pick).astype(BF16)
        total = total + nt(*(jnp.concatenate(blocks, axis=1) for blocks in zip(*pair)))
    base[:, here] = total

    @pl.when(k == pl.num_programs(0) - 1)
    def _():
        over = []
        for b in range(matrix.shape[1] // 256):
            lines = pl.ds(256 * b, 256)
            flow = base[:, lines]
            for a in range(areas):
                inject = jnp.concatenate([held[a, 12], held[a, 13]], axis=1)
                flow = add_flow(flow, inject, matrix, a, lines)
            over.append(excess_of(flow, cap[:, lines]))
        over = jnp.concatenate(over, axis=1)
        excess[...] = over
        for chip in range(areas // 2):
            partial[chip] = nn(over, matrix[2 * chip + 1 - c]).astype(BF16)


def own_side_prices(area, excess, matrix, partial):
    c = lax.rem(area[0], 2)
    for chip in range(partial.shape[0]):
        partial[chip] = nn(excess[...], matrix[2 * chip + c])


def both_sides(mine, other, *more):
    *extra, total = more
    chips = mine.shape[0]
    for chip in range(chips):
        total[chip] = (mine[chip] + other[chip].astype(F32)).astype(BF16)
    for ref in extra:
        for i in range(ref.shape[0]):
            total[chips + i] = ref[i]


def sum_of_four(area, *refs):
    *refs, total = refs
    a, b, c, d = refs
    chips = total.shape[0] if total.shape == a.shape else 2 * len(refs)
    for i in range(chips):
        pairs = (a[i].astype(F32) + b[i].astype(F32)) + (c[i].astype(F32) + d[i].astype(F32))
        total[i] = pairs.astype(BF16)
    count = a.shape[0] - chips
    for bits, ref in enumerate(refs):
        x = lax.bitwise_xor(lax.rem(lax.div(area[0], 2), 4), bits)
        for i in range(count):
            total[chips + count * x + i] = ref[chips + i]


def own_side_flow(area, injection, matrix, base, flow):
    c = lax.rem(area[0], 2)
    for b in range(matrix.shape[1] // 256):
        lines = pl.ds(256 * b, 256)
        total = base[:, lines]
        for chip in range(injection.shape[0]):
            total = add_flow(total, injection[chip], matrix, 2 * chip + c, lines)
        flow[:, lines] = total


def other_side_flow(area, half_flow, mine, other, matrix, imb_base, cap, partial, imbalance, excess, flow):
    c = lax.rem(area[0], 2)
    chips = mine.shape[0]
    over = []
    for b in range(matrix.shape[1] // 256):
        lines = pl.ds(256 * b, 256)
        total = half_flow[:, lines]
        for chip in range(chips):
            total = add_flow(total, other[chip], matrix, 2 * chip + 1 - c, lines)
        flow[:, lines] = total
        over.append(excess_of(total, cap[:, lines]))
    over = jnp.concatenate(over, axis=1)
    excess[...] = over
    if partial.shape[0] == chips:
        for chip in range(chips):
            partial[chip] = nn(over, matrix[2 * chip + 1 - c]).astype(BF16)
    else:
        for a in range(2 * chips):
            partial[a] = nn(over, matrix[a]).astype(BF16)
    total = jnp.zeros(mine.shape[1:], F32)
    for chip in range(chips):
        total += mine[chip].astype(F32) + other[chip].astype(F32)
    imbalance[...] = imb_base[...] + lane_sum(total)


def moved(data, price, imbalance, commit, dispatch, w_comm, w_disp, comm_mean, disp_mean):
    linear, quadratic, fixed_cost, capacity = (data[i : i + 1] for i in range(4))
    grad = (
        linear
        + quadratic * dispatch
        + flow_weight * price
        + imbalance[:, :1] / BUSES
        + w_disp
        + penalty * (dispatch - disp_mean)
    )
    commit = jnp.clip(
        commit - commit_step * (fixed_cost - dispatch / capacity + w_comm + penalty * (commit - comm_mean)), 0.0, 1.0
    )
    step_gen = 1.0 / (quadratic + penalty + 2.0)
    return commit, jnp.clip(dispatch - step_gen * grad, 0.0, capacity * commit)


def summed(prices, at):
    total = prices[(0, *at)].astype(F32)
    for i in range(1, prices.shape[0]):
        total = total + prices[(i, *at)].astype(F32)
    return total


def first_update(near, far, imbalance, data, same, outside_gen, first, commit_out, dispatch_out, injection):
    shape = dispatch_out.shape[1:]
    for chip in range(data.shape[0]):
        values = data[chip]
        start = jnp.broadcast_to(0.25 * values[3:4], shape)
        half = jnp.full(shape, 0.5, F32)
        commit, dispatch = moved(values, near[chip].astype(F32) + far[chip].astype(F32), imbalance, half, start, 0.0, 0.0, half, start)
        commit_out[chip] = commit
        dispatch_out[chip] = dispatch
        injection[chip] = gen_injection(dispatch, same[chip], outside_gen[chip], first[chip])


def second_update(
    area, near, far, imbalance, data, same, outside_gen, first, commit_in, dispatch_in, weight,
    commit_out, dispatch_out, injection, terms, change,
):
    rows = dispatch_in.shape[1]
    for chip in range(data.shape[0]):
        values = data[chip]
        start = jnp.broadcast_to(0.25 * values[3:4], dispatch_in.shape[1:])
        half = jnp.full(start.shape, 0.5, F32)
        commit, dispatch = moved(
            values, near[chip].astype(F32) + far[chip].astype(F32), imbalance, commit_in[chip], dispatch_in[chip], 0.0, 0.0, half, start
        )
        injection[chip] = gen_injection(dispatch, same[chip], outside_gen[chip], first[chip])
        commit_out[chip] = commit
        dispatch_out[chip] = dispatch
    own = lax.div(area[0], 2)
    moves = commit_out[own] - 0.5, dispatch_out[own] - 0.25 * data[own][3:4]
    for i, move in enumerate(moves):
        change[i] = move
        terms[i * rows : (i + 1) * rows] = weight[:1] * move
    terms[2 * rows :] = weight[...]


def sum_terms(refs):
    a, b, c, d = (ref[...].astype(F32) for ref in refs)
    return (a + b) + (c + d)


def add_terms(*refs):
    total = sum_terms(refs[:4])
    for ref in refs[4:]:
        ref[...] = total.astype(ref.dtype)


def mean_kernel(weight, change, terms0, terms1, terms2, terms3, apart, prob):
    total = sum_terms((terms0, terms1, terms2, terms3))
    rows = apart.shape[1]
    weights = total[2 * rows :]
    prob[...] = weight[...] / weights
    for i in range(2):
        apart[i] = (change[i] - total[i * rows : (i + 1) * rows] / weights[:1]).astype(BF16)


def third_update(
    area, near, far, imbalance, data, same, outside_gen, first, commit_in, dispatch_in, state, injection, kept,
):
    chips = data.shape[0]
    for chip in range(chips):
        at = chips + 2 * (chip % 4)
        near_by = lax.div(area[0], 8) == chip // 4
        parts = [jnp.where(near_by, near[at + i].astype(F32), far[at + i].astype(F32)) for i in range(2)]
        commit, dispatch = commit_in[chip], dispatch_in[chip]
        comm_mean, disp_mean = commit - parts[0], dispatch - parts[1]
        w_comm = penalty * parts[0]
        w_disp = penalty * parts[1]
        commit, dispatch = moved(
            data[chip], near[chip].astype(F32) + far[chip].astype(F32), imbalance, commit, dispatch, w_comm, w_disp, comm_mean, disp_mean
        )
        injection[chip] = gen_injection(dispatch, same[chip], outside_gen[chip], first[chip])
        for i, value in enumerate((commit, dispatch, w_comm, w_disp, comm_mean, disp_mean)):
            kept[i, chip] = value
    own = lax.div(area[0], 2)
    for i in range(6):
        state[i] = kept[i, own]


def last_update(area, prices, imbalance, data, state, prob, dispatch_out, terms):
    commit, dispatch = moved(
        data[lax.div(area[0], 2)], summed(prices, ()), imbalance, *(state[i] for i in range(6))
    )
    dispatch_out[...] = dispatch
    rows = commit.shape[0]
    terms[:rows] = prob[:1] * commit
    terms[rows:] = prob[:1] * dispatch


def last_means(terms0, terms1, terms2, terms3, comm_mean, disp_mean):
    total = sum_terms((terms0, terms1, terms2, terms3))
    rows = comm_mean.shape[0]
    comm_mean[...] = total[:rows]
    disp_mean[...] = total[rows:]


def call(kernel, outs, *args, mib=4, cost=1, scalars=0, **more):
    if scalars:
        memories = [pltpu.SMEM] * scalars + [pltpu.VMEM] * (len(args) - scalars)
        more["in_specs"] = [pl.BlockSpec(memory_space=memory) for memory in memories]
    return pl.pallas_call(
        kernel,
        out_shape=[jax.ShapeDtypeStruct(shape, dtype) for shape, dtype in outs],
        compiler_params=pltpu.CompilerParams(vmem_limit_bytes=mib * MIB),
        cost_estimate=pl.CostEstimate(flops=0, transcendentals=0, bytes_accessed=cost * 3_000_000),
        **more,
    )(*args)


def spread(copies, axis, groups=None):
    return lax.all_to_all(copies, axis, split_axis=0, concat_axis=0, tiled=True, axis_index_groups=groups)


def swapped(block, axis, bits):
    return lax.ppermute(block, axis, [(i, i ^ bits) for i in range(lax.axis_size(axis))])


def on_device(wind, load, ptdf_tiles, tile_cols, line_cap, gen_bus, gen_data, prob_weight):
    _, hours, buses = wind.shape
    gens = gen_bus.shape[0]
    lines = line_cap.shape[0]
    areas = lax.axis_size("area")
    scens = lax.axis_size("scen")
    chips = areas // 2
    area = lax.axis_index("area")[None]
    groups = [[2 * i + c for i in range(chips)] for c in range(2)]
    state = (hours, gens)

    [sent] = call(
        prepare_kernel,
        [((chips, 20, hours, 128), BF16)],
        area, wind[0], load, gen_bus[None, :], gen_data,
        mib=56, scalars=1,
    )
    mine = spread(sent, "area", groups)
    other = swapped(mine, "area", 1)
    *params, weight, cols, cap = call(
        params_kernel,
        [
            ((chips, 4, gens), F32),
            ((chips, gens, gens), BF16),
            ((chips, *state), F32),
            ((chips, 1, gens), F32),
            ((8, gens), F32),
            (tile_cols.shape, jnp.int32),
            ((1, lines), F32),
        ],
        prob_weight, mine, tile_cols, line_cap[None, :],
        mib=8, scalars=1,
    )

    def whole(shape):
        return pl.BlockSpec(shape, lambda k: (0,) * len(shape))

    starts = [
        ((areas, lines, gens), BF16),
        ((chips, *state), BF16),
        ((hours, lines), F32),
        ((hours, 128), F32),
        ((hours, 128), F32),
        ((hours, lines), BF16),
    ]
    matrix, partial, base, imb_base, imbalance, excess = call(
        start_kernel,
        starts,
        cols, area, ptdf_tiles, mine, other, cap,
        mib=40, cost=16,
        grid=(ptdf_tiles.shape[0],),
        in_specs=[
            pl.BlockSpec(memory_space=pltpu.SMEM),
            pl.BlockSpec(memory_space=pltpu.SMEM),
            pl.BlockSpec((1, *ptdf_tiles.shape[1:]), lambda k: (k, 0, 0, 0)),
            whole(mine.shape),
            whole(other.shape),
            whole(cap.shape),
        ],
        out_specs=[whole(shape) for shape, _ in starts],
        scratch_shapes=[pltpu.VMEM((areas, 16, hours, 128), BF16), pltpu.VMEM((2, areas, 1, gens), F32)],
    )

    def all_prices(partial, excess, *more):
        theirs = swapped(partial, "area", 1)
        [ours] = call(own_side_prices, [((chips, *state), F32)], area, excess, matrix, cost=2, scalars=1)
        count = sum(a.shape[0] for a in more)
        [total] = call(both_sides, [((chips + count, *state), BF16)], ours, theirs, *more)
        along_x = [swapped(total, "area", bits) for bits in (2, 4, 6)]
        [total] = call(sum_of_four, [((chips + 4 * count, *state), BF16)], area, total, *along_x, scalars=1)
        return total, swapped(total, "area", 8)

    def flow_and_prices(injection, count):
        theirs = swapped(injection, "area", 1)
        [half] = call(own_side_flow, [((hours, lines), F32)], area, injection, matrix, base, cost=2, scalars=1)
        return call(
            other_side_flow,
            [((count, *state), BF16), ((hours, 128), F32), ((hours, lines), BF16), ((hours, lines), F32)],
            area, half, injection, theirs, matrix, imb_base, cap,
            cost=3, scalars=1,
        )

    def near_sum(terms, *dtypes):
        near = [terms] + [swapped(terms, "scen", bits) for bits in (scens // 2, 1, scens // 2 + 1)]
        return call(add_terms, [(terms.shape, dtype) for dtype in dtypes], *near)

    def far_terms(terms):
        return [swapped(terms, "scen", bits) for bits in (2, 4, 6)]

    eight = ((chips, *state), F32)
    eights = [eight, eight, ((chips, *state), BF16)]
    commit, dispatch, injection = call(
        first_update,
        eights,
        *all_prices(partial, excess), imbalance, *params,
        mib=8,
    )
    partial, imbalance, excess, _ = flow_and_prices(injection, chips)
    commit, dispatch, injection, terms, change = call(
        second_update,
        [*eights, ((2 * hours + 8, gens), F32), ((2, *state), F32)],
        area, *all_prices(partial, excess), imbalance, *params, commit, dispatch, weight,
        mib=8, scalars=1,
    )
    near, terms = near_sum(terms, F32, BF16)
    partial, imbalance, excess, _ = flow_and_prices(injection, chips)
    partial, excess, terms = lax.optimization_barrier((partial, excess, terms))
    apart, prob = call(
        mean_kernel,
        [((2, *state), BF16), ((8, gens), F32)],
        weight, change, near, *far_terms(terms),
    )
    kept, injection = call(
        third_update,
        [((6, *state), F32), ((chips, *state), BF16)],
        area, *all_prices(partial, excess, apart), imbalance, *params, commit, dispatch,
        mib=8, scalars=1,
        scratch_shapes=[pltpu.VMEM((6, chips, *state), F32)],
    )
    partial, imbalance, _, flow = flow_and_prices(injection, areas)
    dispatch, terms = call(
        last_update,
        [(state, F32), ((2 * hours, gens), F32)],
        area, spread(partial, "area"), imbalance, params[0], kept, prob,
        scalars=1,
    )
    [terms] = near_sum(terms, F32)
    comm_mean, disp_mean = call(last_means, [(state, F32), (state, F32)], terms, *far_terms(terms))
    return comm_mean, disp_mean, dispatch[None], flow[None]


def solution(mesh):
    placed = (
        P("scen", None, "area"),
        P(None, "area"),
        P("area", None, None, None),
        P("area", None),
        P("area"),
        P("area"),
        P(None, "area"),
        P("scen"),
    )
    return jax.shard_map(
        on_device,
        mesh=mesh,
        in_specs=placed,
        out_specs=(
            P(None, "area"),
            P(None, "area"),
            P("scen", None, "area"),
            P("scen", None, "area"),
        ),
        check_vma=False,
    )
```

```python
import jax
import jax.numpy as jnp
from jax import lax
from jax.experimental import pallas as pl
from jax.experimental.pallas import tpu as pltpu
from jax.sharding import PartitionSpec as P

BUSES = 24576
penalty = 1.0
flow_weight = 0.25
commit_step = 0.5
F32 = jnp.float32
BF16 = jnp.bfloat16
MIB = 1 << 20


def nt(a, b):
    return lax.dot_general(a, b, (((1,), (1,)), ((), ())), preferred_element_type=F32)


def nn(a, b):
    return jnp.dot(a, b, preferred_element_type=F32)


def at_shared_buses(dispatch, same):
    high = dispatch.astype(BF16)
    rest = dispatch - high.astype(F32)
    middle = rest.astype(BF16)
    low = (rest - middle.astype(F32)).astype(BF16)
    return nn(high, same) + (nn(middle, same) + nn(low, same))


def gen_injection(dispatch, same, outside_gen, first):
    placed = at_shared_buses(dispatch, same)
    return jnp.where(first > 0.5, placed + outside_gen, 0.0).astype(BF16)


def first_of(shared):
    gens = shared.shape[0]
    earlier = shared & (
        lax.broadcasted_iota(jnp.int32, (gens, gens), 0) < lax.broadcasted_iota(jnp.int32, (gens, gens), 1)
    )
    return 1.0 - jnp.max(earlier.astype(F32), axis=0, keepdims=True)


def as_column(row):
    return jnp.transpose(jnp.broadcast_to(row, (128, row.shape[1])))[:, :1]


def pieces_of(values):
    high = values.astype(BF16).astype(F32)
    middle = (values - high).astype(BF16).astype(F32)
    return high, middle, values - high - middle


def stacked(lines, rows):
    line = lax.broadcasted_iota(jnp.int32, (rows, lines[0].shape[1]), 0)
    out = jnp.zeros(line.shape, F32)
    for i, values in enumerate(lines):
        out = jnp.where(line == i, values, out)
    return out.astype(BF16)


def prepare_kernel(area, wind, load, bus, data, sent):
    rows, buses = wind.shape
    gens = bus.shape[1]
    row_int = bus[...] - area[0] * buses
    row = row_int.astype(F32)
    col = as_column(row)
    onehot = (col == lax.broadcasted_iota(jnp.int32, (gens, buses), 1).astype(F32)).astype(F32).astype(BF16)
    held = nn(jnp.ones((8, gens), BF16), onehot)[:1]
    wind_gen, load_gen = nt(wind[...], onehot), nt(load[...], onehot)
    shared = col == row
    dispatch = jnp.broadcast_to(0.25 * data[3:4, :], (rows, gens))
    injection = gen_injection(dispatch, shared.astype(F32).astype(BF16), wind_gen - load_gen, first_of(shared))
    base = jnp.where(held > 0.5, 0.0, wind[...].astype(F32) - load[...].astype(F32)).astype(BF16)
    tile_at = row_int // 128
    lane_at = (row_int - 128 * tile_at).astype(F32)
    lines = [tile_at.astype(F32), lane_at]
    for i in range(4):
        lines.extend(pieces_of(data[i : i + 1, :]))
    wind_gen, load_gen = wind_gen.astype(BF16), load_gen.astype(BF16)
    for half in range(2):
        lanes = slice(128 * half, 128 * (half + 1))
        info = stacked([values[:, lanes] for values in lines], rows)
        for copy in range(sent.shape[0]):
            sent[copy, 12 + half] = injection[:, lanes]
            sent[copy, 14 + half] = info
            sent[copy, 16 + half] = wind_gen[:, lanes]
            sent[copy, 18 + half] = load_gen[:, lanes]
    for copy in range(sent.shape[0]):
        for j in range(12):
            sent[copy, j] = base[:, 128 * j : 128 * (j + 1)]


def side_by_side(blocks, *at):
    left, right = blocks[at].astype(F32), blocks[(*at[:-1], at[-1] + 1)].astype(F32)
    return jnp.concatenate([left, right], axis=1)


def params_kernel(prob_weight, mine, cols, cap, data, same, outside_gen, first, weight, cols_out, cap_out):
    cols_out[...] = cols[...]
    cap_out[...] = cap[...]
    weight[...] = jnp.full(weight.shape, prob_weight[0].astype(F32))
    for chip in range(mine.shape[0]):
        info = side_by_side(mine, chip, 14)
        bus = info[0:1] * 128.0 + info[1:2]
        shared = as_column(bus) == bus
        same[chip] = shared.astype(F32).astype(BF16)
        first[chip] = first_of(shared)
        for i in range(4):
            at = 2 + 3 * i
            data[chip, i : i + 1] = info[at : at + 1] + info[at + 1 : at + 2] + info[at + 2 : at + 3]
        outside_gen[chip] = side_by_side(mine, chip, 16) - side_by_side(mine, chip, 18)


def add_flow(total, inject, matrix, area, rows):
    return total + nt(inject, matrix[area, rows, :])


def excess_of(flow, limit):
    return (flow - jnp.clip(flow, -limit, limit)).astype(BF16)


def lane_sum(total):
    return jnp.broadcast_to(jnp.sum(total, axis=1, keepdims=True), (total.shape[0], 128))


def start_kernel(
    cols, area, tiles, mine, other, cap,
    matrix, partial, base, imb_base, imbalance, excess, held, code,
):
    k = pl.program_id(0)
    areas = matrix.shape[0]
    rows = held.shape[2]
    c = lax.rem(area[0], 2)

    @pl.when(k == 0)
    def _():
        for chip in range(areas // 2):
            for j in range(16):
                held[2 * chip + c, j] = mine[chip, j]
                held[2 * chip + 1 - c, j] = other[chip, j]
        total = jnp.zeros((rows, 128), F32)
        gen_total = jnp.zeros((rows, 128), F32)
        for a in range(areas):
            for j in range(12):
                total += held[a, j].astype(F32)
            for j in range(12, 14):
                gen_total += held[a, j].astype(F32)
            info = side_by_side(held, a, 14)
            code[0, a] = info[0:1]
            code[1, a] = info[1:2]
        before = lane_sum(total)
        imb_base[...] = before
        imbalance[...] = before + lane_sum(gen_total)
        matrix[...] = jnp.zeros_like(matrix)

    at_bus = lax.broadcasted_iota(jnp.int32, (128, 256), 0).astype(F32).astype(BF16)
    one, zero = jnp.ones((128, 256), BF16), jnp.zeros((128, 256), BF16)
    here = pl.ds(pl.multiple_of(k * 128, 128), 128)

    total = jnp.zeros((rows, 128), F32)
    for z in range(0, tiles.shape[1], 4):
        pair = []
        for slot in range(z, z + 4):
            t = cols[k, slot]
            a = t // 12
            j = t - 12 * a
            tile = tiles[0, slot]
            pair.append((held[a, j], tile))
            bus = jnp.where(code[0, a] == j.astype(F32), code[1, a], 255.0).astype(BF16)
            pick = jnp.where(at_bus == bus, one, zero)
            matrix[a, here, :] = matrix[a, here, :] + nn(tile, pick).astype(BF16)
        total = total + nt(*(jnp.concatenate(blocks, axis=1) for blocks in zip(*pair)))
    base[:, here] = total

    @pl.when(k == pl.num_programs(0) - 1)
    def _():
        over = []
        for b in range(matrix.shape[1] // 256):
            lines = pl.ds(256 * b, 256)
            flow = base[:, lines]
            for a in range(areas):
                inject = jnp.concatenate([held[a, 12], held[a, 13]], axis=1)
                flow = add_flow(flow, inject, matrix, a, lines)
            over.append(excess_of(flow, cap[:, lines]))
        over = jnp.concatenate(over, axis=1)
        excess[...] = over
        for chip in range(areas // 2):
            partial[chip] = nn(over, matrix[2 * chip + 1 - c]).astype(BF16)


def own_side_prices(area, excess, matrix, partial):
    c = lax.rem(area[0], 2)
    for chip in range(partial.shape[0]):
        partial[chip] = nn(excess[...], matrix[2 * chip + c])


def both_sides(mine, other, *more):
    *extra, total = more
    chips = mine.shape[0]
    for chip in range(chips):
        total[chip] = (mine[chip] + other[chip].astype(F32)).astype(BF16)
    for ref in extra:
        for i in range(ref.shape[0]):
            total[chips + i] = ref[i]


def sum_of_four(area, *refs):
    *refs, total = refs
    a, b, c, d = refs
    chips = total.shape[0] if total.shape == a.shape else 2 * len(refs)
    for i in range(chips):
        pairs = (a[i].astype(F32) + b[i].astype(F32)) + (c[i].astype(F32) + d[i].astype(F32))
        total[i] = pairs.astype(BF16)
    count = a.shape[0] - chips
    for bits, ref in enumerate(refs):
        x = lax.bitwise_xor(lax.rem(lax.div(area[0], 2), 4), bits)
        for i in range(count):
            total[chips + count * x + i] = ref[chips + i]


def own_side_flow(area, injection, matrix, base, flow):
    c = lax.rem(area[0], 2)
    for b in range(matrix.shape[1] // 256):
        lines = pl.ds(256 * b, 256)
        total = base[:, lines]
        for chip in range(injection.shape[0]):
            total = add_flow(total, injection[chip], matrix, 2 * chip + c, lines)
        flow[:, lines] = total


def other_side_flow(area, half_flow, mine, other, matrix, imb_base, cap, partial, imbalance, excess, flow):
    c = lax.rem(area[0], 2)
    chips = mine.shape[0]
    over = []
    for b in range(matrix.shape[1] // 256):
        lines = pl.ds(256 * b, 256)
        total = half_flow[:, lines]
        for chip in range(chips):
            total = add_flow(total, other[chip], matrix, 2 * chip + 1 - c, lines)
        flow[:, lines] = total
        over.append(excess_of(total, cap[:, lines]))
    over = jnp.concatenate(over, axis=1)
    excess[...] = over
    if partial.shape[0] == chips:
        for chip in range(chips):
            partial[chip] = nn(over, matrix[2 * chip + 1 - c]).astype(BF16)
    else:
        for a in range(2 * chips):
            partial[a] = nn(over, matrix[a]).astype(BF16)
    total = jnp.zeros(mine.shape[1:], F32)
    for chip in range(chips):
        total += mine[chip].astype(F32) + other[chip].astype(F32)
    imbalance[...] = imb_base[...] + lane_sum(total)


def moved(data, price, imbalance, commit, dispatch, w_comm, w_disp, comm_mean, disp_mean):
    linear, quadratic, fixed_cost, capacity = (data[i : i + 1] for i in range(4))
    grad = (
        linear
        + quadratic * dispatch
        + flow_weight * price
        + imbalance[:, :1] / BUSES
        + w_disp
        + penalty * (dispatch - disp_mean)
    )
    commit = jnp.clip(
        commit - commit_step * (fixed_cost - dispatch / capacity + w_comm + penalty * (commit - comm_mean)), 0.0, 1.0
    )
    step_gen = 1.0 / (quadratic + penalty + 2.0)
    return commit, jnp.clip(dispatch - step_gen * grad, 0.0, capacity * commit)


def summed(prices, at):
    total = prices[(0, *at)].astype(F32)
    for i in range(1, prices.shape[0]):
        total = total + prices[(i, *at)].astype(F32)
    return total


def first_update(near, far, imbalance, data, same, outside_gen, first, commit_out, dispatch_out, injection):
    shape = dispatch_out.shape[1:]
    for chip in range(data.shape[0]):
        values = data[chip]
        start = jnp.broadcast_to(0.25 * values[3:4], shape)
        half = jnp.full(shape, 0.5, F32)
        commit, dispatch = moved(values, near[chip].astype(F32) + far[chip].astype(F32), imbalance, half, start, 0.0, 0.0, half, start)
        commit_out[chip] = commit
        dispatch_out[chip] = dispatch
        injection[chip] = gen_injection(dispatch, same[chip], outside_gen[chip], first[chip])


def second_update(
    area, near, far, imbalance, data, same, outside_gen, first, commit_in, dispatch_in, weight,
    commit_out, dispatch_out, injection, terms, change,
):
    rows = dispatch_in.shape[1]
    for chip in range(data.shape[0]):
        values = data[chip]
        start = jnp.broadcast_to(0.25 * values[3:4], dispatch_in.shape[1:])
        half = jnp.full(start.shape, 0.5, F32)
        commit, dispatch = moved(
            values, near[chip].astype(F32) + far[chip].astype(F32), imbalance, commit_in[chip], dispatch_in[chip], 0.0, 0.0, half, start
        )
        injection[chip] = gen_injection(dispatch, same[chip], outside_gen[chip], first[chip])
        commit_out[chip] = commit
        dispatch_out[chip] = dispatch
    own = lax.div(area[0], 2)
    moves = commit_out[own] - 0.5, dispatch_out[own] - 0.25 * data[own][3:4]
    for i, move in enumerate(moves):
        change[i] = move
        terms[i * rows : (i + 1) * rows] = weight[:1] * move
    terms[2 * rows :] = weight[...]


def sum_terms(refs):
    a, b, c, d = (ref[...].astype(F32) for ref in refs)
    return (a + b) + (c + d)


def add_terms(*refs):
    total = sum_terms(refs[:4])
    for ref in refs[4:]:
        ref[...] = total.astype(ref.dtype)


def mean_kernel(weight, change, terms0, terms1, terms2, terms3, apart, prob):
    total = sum_terms((terms0, terms1, terms2, terms3))
    rows = apart.shape[1]
    weights = total[2 * rows :]
    prob[...] = weight[...] / weights
    for i in range(2):
        apart[i] = (change[i] - total[i * rows : (i + 1) * rows] / weights[:1]).astype(BF16)


def third_update(
    area, near, far, imbalance, data, same, outside_gen, first, commit_in, dispatch_in, state, injection, kept,
):
    chips = data.shape[0]
    for chip in range(chips):
        at = chips + 2 * (chip % 4)
        near_by = lax.div(area[0], 8) == chip // 4
        parts = [jnp.where(near_by, near[at + i].astype(F32), far[at + i].astype(F32)) for i in range(2)]
        commit, dispatch = commit_in[chip], dispatch_in[chip]
        comm_mean, disp_mean = commit - parts[0], dispatch - parts[1]
        w_comm = penalty * parts[0]
        w_disp = penalty * parts[1]
        commit, dispatch = moved(
            data[chip], near[chip].astype(F32) + far[chip].astype(F32), imbalance, commit, dispatch, w_comm, w_disp, comm_mean, disp_mean
        )
        injection[chip] = gen_injection(dispatch, same[chip], outside_gen[chip], first[chip])
        for i, value in enumerate((commit, dispatch, w_comm, w_disp, comm_mean, disp_mean)):
            kept[i, chip] = value
    own = lax.div(area[0], 2)
    for i in range(6):
        state[i] = kept[i, own]


def last_update(area, prices, imbalance, data, state, prob, dispatch_out, terms):
    commit, dispatch = moved(
        data[lax.div(area[0], 2)], summed(prices, ()), imbalance, *(state[i] for i in range(6))
    )
    dispatch_out[...] = dispatch
    rows = commit.shape[0]
    terms[:rows] = prob[:1] * commit
    terms[rows:] = prob[:1] * dispatch


def last_means(terms0, terms1, terms2, terms3, comm_mean, disp_mean):
    total = sum_terms((terms0, terms1, terms2, terms3))
    rows = comm_mean.shape[0]
    comm_mean[...] = total[:rows]
    disp_mean[...] = total[rows:]


def call(kernel, outs, *args, mib=4, cost=1, scalars=0, **more):
    if scalars:
        memories = [pltpu.SMEM] * scalars + [pltpu.VMEM] * (len(args) - scalars)
        more["in_specs"] = [pl.BlockSpec(memory_space=memory) for memory in memories]
    return pl.pallas_call(
        kernel,
        out_shape=[jax.ShapeDtypeStruct(shape, dtype) for shape, dtype in outs],
        compiler_params=pltpu.CompilerParams(vmem_limit_bytes=mib * MIB),
        cost_estimate=pl.CostEstimate(flops=0, transcendentals=0, bytes_accessed=cost * 3_000_000),
        **more,
    )(*args)


def spread(copies, axis, groups=None):
    return lax.all_to_all(copies, axis, split_axis=0, concat_axis=0, tiled=True, axis_index_groups=groups)


def swapped(block, axis, bits):
    return lax.ppermute(block, axis, [(i, i ^ bits) for i in range(lax.axis_size(axis))])


def on_device(wind, load, ptdf_tiles, tile_cols, line_cap, gen_bus, gen_data, prob_weight):
    _, hours, buses = wind.shape
    gens = gen_bus.shape[0]
    lines = line_cap.shape[0]
    areas = lax.axis_size("area")
    scens = lax.axis_size("scen")
    chips = areas // 2
    area = lax.axis_index("area")[None]
    groups = [[2 * i + c for i in range(chips)] for c in range(2)]
    state = (hours, gens)

    [sent] = call(
        prepare_kernel,
        [((chips, 20, hours, 128), BF16)],
        area, wind[0], load, gen_bus[None, :], gen_data,
        mib=56, scalars=1,
    )
    mine = spread(sent, "area", groups)
    other = swapped(mine, "area", 1)
    *params, weight, cols, cap = call(
        params_kernel,
        [
            ((chips, 4, gens), F32),
            ((chips, gens, gens), BF16),
            ((chips, *state), F32),
            ((chips, 1, gens), F32),
            ((8, gens), F32),
            (tile_cols.shape, jnp.int32),
            ((1, lines), F32),
        ],
        prob_weight, mine, tile_cols, line_cap[None, :],
        mib=8, scalars=1,
    )

    def whole(shape):
        return pl.BlockSpec(shape, lambda k: (0,) * len(shape))

    starts = [
        ((areas, lines, gens), BF16),
        ((chips, *state), BF16),
        ((hours, lines), F32),
        ((hours, 128), F32),
        ((hours, 128), F32),
        ((hours, lines), BF16),
    ]
    matrix, partial, base, imb_base, imbalance, excess = call(
        start_kernel,
        starts,
        cols, area, ptdf_tiles, mine, other, cap,
        mib=40, cost=16,
        grid=(ptdf_tiles.shape[0],),
        in_specs=[
            pl.BlockSpec(memory_space=pltpu.SMEM),
            pl.BlockSpec(memory_space=pltpu.SMEM),
            pl.BlockSpec((1, *ptdf_tiles.shape[1:]), lambda k: (k, 0, 0, 0)),
            whole(mine.shape),
            whole(other.shape),
            whole(cap.shape),
        ],
        out_specs=[whole(shape) for shape, _ in starts],
        scratch_shapes=[pltpu.VMEM((areas, 16, hours, 128), BF16), pltpu.VMEM((2, areas, 1, gens), F32)],
    )

    def all_prices(partial, excess, *more):
        theirs = swapped(partial, "area", 1)
        [ours] = call(own_side_prices, [((chips, *state), F32)], area, excess, matrix, cost=2, scalars=1)
        count = sum(a.shape[0] for a in more)
        [total] = call(both_sides, [((chips + count, *state), BF16)], ours, theirs, *more)
        along_x = [swapped(total, "area", bits) for bits in (2, 4, 6)]
        [total] = call(sum_of_four, [((chips + 4 * count, *state), BF16)], area, total, *along_x, scalars=1)
        return total, swapped(total, "area", 8)

    def flow_and_prices(injection, count):
        theirs = swapped(injection, "area", 1)
        [half] = call(own_side_flow, [((hours, lines), F32)], area, injection, matrix, base, cost=2, scalars=1)
        return call(
            other_side_flow,
            [((count, *state), BF16), ((hours, 128), F32), ((hours, lines), BF16), ((hours, lines), F32)],
            area, half, injection, theirs, matrix, imb_base, cap,
            cost=3, scalars=1,
        )

    def near_sum(terms, *dtypes):
        near = [terms] + [swapped(terms, "scen", bits) for bits in (scens // 2, 1, scens // 2 + 1)]
        return call(add_terms, [(terms.shape, dtype) for dtype in dtypes], *near)

    def far_terms(terms):
        return [swapped(terms, "scen", bits) for bits in (2, 4, 6)]

    eight = ((chips, *state), F32)
    eights = [eight, eight, ((chips, *state), BF16)]
    commit, dispatch, injection = call(
        first_update,
        eights,
        *all_prices(partial, excess), imbalance, *params,
        mib=8,
    )
    partial, imbalance, excess, _ = flow_and_prices(injection, chips)
    commit, dispatch, injection, terms, change = call(
        second_update,
        [*eights, ((2 * hours + 8, gens), F32), ((2, *state), F32)],
        area, *all_prices(partial, excess), imbalance, *params, commit, dispatch, weight,
        mib=8, scalars=1,
    )
    near, terms = near_sum(terms, F32, BF16)
    partial, imbalance, excess, _ = flow_and_prices(injection, chips)
    partial, excess, terms = lax.optimization_barrier((partial, excess, terms))
    apart, prob = call(
        mean_kernel,
        [((2, *state), BF16), ((8, gens), F32)],
        weight, change, near, *far_terms(terms),
    )
    kept, injection = call(
        third_update,
        [((6, *state), F32), ((chips, *state), BF16)],
        area, *all_prices(partial, excess, apart), imbalance, *params, commit, dispatch,
        mib=8, scalars=1,
        scratch_shapes=[pltpu.VMEM((6, chips, *state), F32)],
    )
    partial, imbalance, _, flow = flow_and_prices(injection, areas)
    dispatch, terms = call(
        last_update,
        [(state, F32), ((2 * hours, gens), F32)],
        area, spread(partial, "area"), imbalance, params[0], kept, prob,
        scalars=1,
    )
    [terms] = near_sum(terms, F32)
    comm_mean, disp_mean = call(last_means, [(state, F32), (state, F32)], terms, *far_terms(terms))
    return comm_mean, disp_mean, dispatch[None], flow[None]


def solution(mesh):
    placed = (
        P("scen", None, "area"),
        P(None, "area"),
        P("area", None, None, None),
        P("area", None),
        P("area"),
        P("area"),
        P(None, "area"),
        P("scen"),
    )
    return jax.shard_map(
        on_device,
        mesh=mesh,
        in_specs=placed,
        out_specs=(
            P(None, "area"),
            P(None, "area"),
            P("scen", None, "area"),
            P("scen", None, "area"),
        ),
        check_vma=False,
    )
```
